128 devices in a mesh: ctx: 64 (over y, x, z), head: 2 (over core).
Axes of the slice: x: 4, y: 4, z: 4, core: 2. Of those that a mesh axis runs over, the one named last changes fastest.
Arguments:
- hidden: bfloat16 [16384, 4096], P('ctx', 'head'), may hold values from -6 to 6
- block_owner: int32 [128], replicated, may hold values from 0 to 63, as said below
- doc_lengths: int32 [32], replicated, may hold values from 1 to 1024, 16384 in all
- w_query: bfloat16 [4096, 2048], P(None, 'head'), may hold values from -1 to 1
- w_key: bfloat16 [4096, 512], P(None, 'head'), may hold values from -1 to 1
- value_weight: bfloat16 [4096, 512], P(None, 'head'), may hold values from -0.09375 to 0.09375
Outputs:
- attended: bfloat16 [16384, 2048], P('ctx', 'head')
The draws below stay inside these ranges and needn't reach their ends.
Inputs may be any that keep to these rules, and one draw needn't show every extreme that they name: `block_owner`: owners never fall along the blocks; context shard j holds a run of blocks (possibly empty) that starts within 1 block of block j * 2, shard 0 at block 0; so a block's owner is its loader shard or a neighbour. Shard 1 starts exactly 1 block early and shard 2 starts late. Some shard holds exactly 4 blocks. `doc_lengths`: the lengths sum to 16384; the longest is exactly 1024.
All inputs are finite; a program needn't handle non-finite values.
Results may differ from the reference program's by a relative error of at most 0.008.
Values may be sent and summed in bfloat16 or wider, within the bound.
A program may use at most 128 MiB of HBM per device.

```python
import math
import jax
import jax.numpy as jnp
import numpy as np
from jax import lax

MODEL_WIDTH = 4096
QUERY_HEADS = 16
KEY_VALUE_HEADS = 4
HEAD_SIZE_DIM = 128
BLK = 128
REACH = 2
TOK_DEV = 256
TOKENS = 16384
BLOCKS = 128
NDOCS = 32


def projection_pair(key):
    key = jax.random.fold_in(key, 41)
    first_key, later_key = jax.random.split(key)
    weight_scaling = 1.0 / math.sqrt(MODEL_WIDTH)
    query_part = jnp.clip(jax.random.normal(first_key, (MODEL_WIDTH, QUERY_HEADS * HEAD_SIZE_DIM), jnp.float32), -6.0, 6.0) * weight_scaling
    key_portion = jnp.clip(jax.random.normal(later_key, (MODEL_WIDTH, KEY_VALUE_HEADS * HEAD_SIZE_DIM), jnp.float32), -6.0, 6.0) * weight_scaling
    return (query_part, key_portion)


def draw_w_query(key, part):
    paired = projection_pair(key)
    return paired[0].astype(jnp.bfloat16)


def draw_w_key(key, part):
    paired = projection_pair(key)
    return paired[1].astype(jnp.bfloat16)


def draw_hidden(key, part):
    key = jax.random.fold_in(key, 5)
    key_list = jax.random.split(key, 1)
    normal_rows = jnp.clip(jax.random.normal(key_list[0], (TOKENS, MODEL_WIDTH), jnp.float32), -6.0, 6.0)
    return normal_rows.astype(jnp.bfloat16)


def draw_block_owner(key, part):
    key = jax.random.fold_in(key, 7)
    per_shard = TOK_DEV // BLK
    half = per_shard // 2
    shards = BLOCKS // per_shard
    first_key, later_key, third_key = jax.random.split(key, 3)
    edge = jax.random.randint(first_key, (shards + 1,), -half, half + 1)
    late_start = jax.random.randint(third_key, (), 1, half + 1)
    spot = jax.random.randint(later_key, (), 3, shards - 1)
    index = jnp.arange(shards + 1)
    edge = jnp.where(index == 1, -half, edge)
    edge = jnp.where(index == 2, late_start, edge)
    edge = jnp.where(index == spot, -half, edge)
    edge = jnp.where(index == spot + 1, half, edge)
    edge = jnp.where((index == 0) | (index == shards), 0, edge)
    begins = index * per_shard + edge
    blocks = jnp.arange(BLOCKS)
    inner = begins[1:shards]
    owner = jnp.sum((inner[None, :] <= blocks[:, None]).astype(jnp.int32), axis=1)
    return owner.astype(jnp.int32)


def block_scale(own_key, dims, pieces, smallest, high):
    factor_of = 1.0
    for dim, shards_of in pieces:
        steps = jax.random.uniform(jax.random.fold_in(jax.random.fold_in(own_key, 6), dim), (shards_of,), jnp.float32, smallest / len(pieces), high / len(pieces))
        factor_of = factor_of * jnp.repeat(jnp.exp(steps), dims[dim] // shards_of).reshape((-1,) + (1,) * (len(dims) - 1 - dim))
    return factor_of


def profile(amount, total, most, slope):
    portions = [(1 << 20) // math.isqrt(standing ** slope) + 1 for standing in range(2, amount + 1)]
    rest, given = total - most - (amount - 1), [1] * (amount - 1)
    while rest > 0:
        movable = [i for i in range(amount - 1) if given[i] < most]
        pool, remaining = sum([portions[i] for i in movable]), rest
        for i in movable:
            addition = min(most - given[i], max(1, remaining * portions[i] // pool), rest)
            given[i] = given[i] + addition
            rest = rest - addition
    return np.array([most] + given)


def uneven_parts(stream_key, count, total, limit, slope):
    if count == 2:
        one = jax.random.randint(stream_key, (), max(1, total - limit), min(limit, total - 1) + 1)
        return jnp.stack([one, total - one])
    lengths = jnp.asarray(profile(count, total, limit, slope), jnp.int32)
    couples = (count - 1) // 2
    source_of, sink = lengths[1:1 + 2 * couples:2], lengths[2:2 + 2 * couples:2]
    margin = jnp.minimum(source_of - 1, limit - sink)
    shifted = jax.random.randint(jax.random.fold_in(stream_key, 1), (couples,), 0, 1 << 20) % (margin + 1)
    lengths = lengths.at[1:1 + 2 * couples:2].set(source_of - shifted).at[2:2 + 2 * couples:2].set(sink + shifted)
    return lengths[jax.random.permutation(jax.random.fold_in(stream_key, 2), count)]


def centred(key, shape, scale, limit, cuts=(), kind=jnp.bfloat16):
    gain = block_scale(key, shape, cuts, -0.22, 0.18) if cuts else 1.0
    drawn = jax.random.normal(key, shape, jnp.float32) * scale * gain
    return jnp.minimum(jnp.maximum(drawn, -limit), limit).astype(kind)


def setup_inputs(seed: int = 0) -> dict:
    seeds = jax.random.split(jax.random.key(seed), 7)
    return {
        "hidden": draw_hidden(jax.random.fold_in(seeds[6], 71), 0),
        "block_owner": draw_block_owner(jax.random.fold_in(seeds[6], 71), 0),
        "doc_lengths": uneven_parts(seeds[2], NDOCS, TOKENS, 4 * TOK_DEV, 1).astype(jnp.int32),
        "w_query": draw_w_query(jax.random.fold_in(seeds[6], 71), 0),
        "w_key": draw_w_key(jax.random.fold_in(seeds[6], 71), 0),
        "value_weight": centred(seeds[5], (MODEL_WIDTH, KEY_VALUE_HEADS * HEAD_SIZE_DIM), MODEL_WIDTH ** -0.5, 0.09375, ((1, 2),)),
    }


def reference(hidden, block_owner, doc_lengths, w_query, w_key, value_weight):
    query_matrix = jnp.dot(hidden, w_query, preferred_element_type=jnp.float32).astype(jnp.bfloat16)
    key_matrix = jnp.dot(hidden, w_key, preferred_element_type=jnp.float32).astype(jnp.bfloat16)
    value_matrix = jnp.dot(hidden, value_weight, preferred_element_type=jnp.float32).astype(jnp.bfloat16)
    head_group = QUERY_HEADS // KEY_VALUE_HEADS
    position = jnp.arange(TOKENS, dtype=jnp.int32)
    owner = jnp.repeat(block_owner, BLK)
    low_blocks = jnp.sum((block_owner[None, :] < (owner - REACH)[:, None]).astype(jnp.int32), axis=1)
    ends = jnp.cumsum(doc_lengths).astype(jnp.int32)
    doc_start = jnp.sum(doc_lengths[None, :] * (ends[None, :] <= position[:, None]).astype(jnp.int32), axis=1)
    lower = jnp.maximum(doc_start, low_blocks * BLK).astype(jnp.int32)
    attention_window = (REACH + 1) * 2 * TOK_DEV
    query_block = 512
    key_padding = jnp.concatenate([jnp.zeros((attention_window, KEY_VALUE_HEADS * HEAD_SIZE_DIM), jnp.bfloat16), key_matrix], axis=0)
    value_padding = jnp.concatenate([jnp.zeros((attention_window, KEY_VALUE_HEADS * HEAD_SIZE_DIM), jnp.bfloat16), value_matrix], axis=0)
    scale = 1.0 / (HEAD_SIZE_DIM ** 0.5)

    def one_block(start_position):
        start_position = start_position.astype(jnp.int32)
        query_row_set = lax.dynamic_slice_in_dim(query_matrix, start_position, query_block, 0).reshape(query_block, KEY_VALUE_HEADS, head_group, HEAD_SIZE_DIM)
        key_row_set = lax.dynamic_slice_in_dim(key_padding, start_position, attention_window + query_block, 0).reshape(attention_window + query_block, KEY_VALUE_HEADS, HEAD_SIZE_DIM)
        value_row_set = lax.dynamic_slice_in_dim(value_padding, start_position, attention_window + query_block, 0).reshape(attention_window + query_block, KEY_VALUE_HEADS, HEAD_SIZE_DIM)
        query_pos = start_position + jnp.arange(query_block, dtype=jnp.int32)
        key_pos = start_position - attention_window + jnp.arange(attention_window + query_block, dtype=jnp.int32)
        bound = lax.dynamic_slice_in_dim(lower, start_position, query_block, 0)
        allowed = (key_pos[None, :] >= bound[:, None]) & (key_pos[None, :] <= query_pos[:, None])
        scores = jnp.einsum("qhgd,khd->hgqk", query_row_set.astype(jnp.float32), key_row_set.astype(jnp.float32)) * scale
        scores = jnp.where(allowed[None, None], scores, jnp.float32(-1e30))
        largest = jnp.max(scores, axis=-1, keepdims=True)
        expo = jnp.exp(scores - largest)
        total = jnp.sum(expo, axis=-1, keepdims=True)
        weights = expo.astype(jnp.bfloat16)
        mixed = jnp.einsum("hgqk,khd->hgqd", weights.astype(jnp.float32), value_row_set.astype(jnp.float32)) / total
        return jnp.transpose(mixed, (2, 0, 1, 3)).reshape(query_block, QUERY_HEADS * HEAD_SIZE_DIM).astype(jnp.bfloat16)

    starts = jnp.arange(TOKENS // query_block, dtype=jnp.int32) * query_block
    blocks_out = lax.map(one_block, starts)
    return blocks_out.reshape(TOKENS, QUERY_HEADS * HEAD_SIZE_DIM)
```

```python
import functools
import math

import jax
import jax.numpy as jnp
from jax import lax
from jax.experimental import pallas as pl
from jax.experimental.pallas import tpu as pltpu
from jax.sharding import PartitionSpec as P

HEAD = 128
BLK = 128
REACH = 2
NEG = -1e30
MESH = pl.DeviceIdType.MESH
OWN, BACK1, BACK3, BACK2, BACK4, PASS_UP, PASS_DOWN, PASS_ROW = range(8)
NT = (((1,), (1,)), ((), ()))


def kernel(
    shards,
    hid,
    owner,
    lengths,
    w_q,
    w_k,
    w_v,
    out,
    h_own,
    h_oth,
    wq,
    wk,
    wv,
    kv_sum,
    q_sum,
    qs,
    kv,
    low_row,
    pos_row,
    m_s,
    l_s,
    acc_s,
    load_sem,
    hid_send,
    hid_recv,
    send_sem,
    recv_sem,
):
    here = lax.axis_index("ctx")
    head = lax.axis_index("head")
    z = lax.rem(here, 4)
    ring = here - z
    up = ring + lax.rem(z + 1, 4)
    down = ring + lax.rem(z + 3, 4)
    row_next = lax.rem(here + 4, shards)
    row_prev = lax.rem(here + shards - 4, shards)
    half = h_own.shape[1]
    mine = pl.multiple_of(head * half, half)
    other = pl.multiple_of((1 - head) * half, half)

    loads = [pltpu.make_async_copy(hid, h_own, load_sem.at[0])]
    for part, first in ((0, mine), (1, other)):
        for src, dst in ((w_k, wk), (w_v, wv)):
            loads.append(
                pltpu.make_async_copy(
                    src.at[pl.ds(first, half)], dst.at[part], load_sem.at[len(loads)]
                )
            )
    for part, first in ((0, mine), (1, other)):
        loads.append(
            pltpu.make_async_copy(
                w_q.at[pl.ds(first, half)], wq.at[part], load_sem.at[len(loads)]
            )
        )
    for load in loads:
        load.start()
    load_h, load_k0, load_v0, load_k1, load_v1, load_q0, load_q1 = loads

    barrier = pltpu.get_barrier_semaphore()
    for peer in ((here, 1 - head), (up, head), (down, head), (row_prev, head)):
        pl.semaphore_signal(barrier, inc=1, device_id=peer, device_id_type=MESH)
    pl.semaphore_wait(barrier, 4)

    swaps = []
    for blk in range(2):
        rows = pl.ds(blk * BLK, BLK)
        swaps.append(
            pltpu.make_async_remote_copy(
                src_ref=hid.at[rows],
                dst_ref=h_oth.at[rows],
                send_sem=hid_send.at[blk],
                recv_sem=hid_recv.at[blk],
                device_id=(here, 1 - head),
                device_id_type=MESH,
            )
        )
        swaps[-1].start()

    first_block = 2 * here - 8
    lane = lax.broadcasted_iota(jnp.int32, (8, BLK), 1)
    for blk in range(2):
        shard = owner[2 * here + blk]
        low = jnp.maximum(first_block, 0)
        for j in range(10):
            block = first_block + j
            below = owner[jnp.maximum(block, 0)] < shard - REACH
            low = low + jnp.where(below & (block >= 0), 1, 0)
        pos = (2 * here + blk) * BLK + lane
        start = jnp.int32(0)
        doc = jnp.zeros((8, BLK), jnp.int32)
        for i in range(lengths.shape[0]):
            doc = jnp.where(pos >= start, start, doc)
            start = start + lengths[i]
        lower = jnp.maximum(doc, low * BLK)
        for hh in range(4):
            cols = slice((blk * 4 + hh) * BLK, (blk * 4 + hh + 1) * BLK)
            low_row[:, cols] = lower
            pos_row[:, cols] = pos

    def copy(src, dst, piece, to, k):
        return pltpu.make_async_remote_copy(
            src_ref=kv.at[src, piece],
            dst_ref=kv.at[dst, piece],
            send_sem=send_sem.at[k],
            recv_sem=recv_sem.at[dst, piece],
            device_id=(to, head),
            device_id_type=MESH,
        )

    sends = [0, 0, 0, 0]
    waited = [set(), set(), set(), set()]

    def send(col, src, dst, piece, to):
        copy(src, dst, piece, to, sends[col]).start()
        sends[col] += 1

    def arrive(col, slot, piece):
        if (slot, piece) not in waited[col]:
            waited[col].add((slot, piece))
            copy(OWN, slot, piece, up, 0).wait_recv()

    def by_column(step):
        for col in range(4):
            pl.when(z == col)(functools.partial(step, col))

    A, B = (0, 1), (2, 3)

    def send_first(col):
        for a in A:
            send(col, OWN, BACK1 if col < 3 else PASS_UP, a, up)
            send(col, OWN, PASS_DOWN if col > 0 else BACK3, a, down)

    def send_second(col):
        for b in B:
            send(col, OWN, BACK4, b, row_next)
            if col < 3:
                send(col, OWN, BACK1, b, up)
            if col == 0:
                send(col, OWN, BACK3, b, down)

    def relay_first(i, col):
        a, b = A[i], B[i]
        if col == 0:
            arrive(col, PASS_DOWN, a)
            send(col, PASS_DOWN, BACK3, a, row_next)
            send(col, PASS_DOWN, BACK2, a, down)
            arrive(col, PASS_UP, a)
            send(col, PASS_UP, BACK1, a, row_next)
        if col in (1, 2):
            arrive(col, PASS_DOWN, a)
            send(col, PASS_DOWN, BACK3, a, row_next)
        if col == 1:
            arrive(col, BACK1, a)
            send(col, BACK1, BACK2, a, up)
        if col == 3:
            arrive(col, BACK1, a)
            send(col, BACK1, PASS_ROW, a, row_next)
        if col > 0:
            arrive(col, BACK4, b)
            send(col, BACK4, BACK3, b, down)
        if col == 3:
            send(col, BACK4, BACK1, b, up)

    def relay_second(i, col):
        b = B[i]
        if col == 2:
            arrive(col, BACK1, b)
            send(col, BACK1, BACK2, b, up)
        if col == 3:
            arrive(col, BACK3, b)
            send(col, BACK3, BACK2, b, down)

    def relay_third(i, col):
        a, b = A[i], B[i]
        if col == 0:
            arrive(col, BACK1, b)
            send(col, BACK1, BACK2, b, up)
        if col == 1:
            arrive(col, BACK3, b)
            send(col, BACK3, BACK2, b, down)
        if col == 2:
            arrive(col, BACK3, a)
            send(col, BACK3, BACK2, a, down)
        if col == 3:
            arrive(col, PASS_ROW, a)
            send(col, PASS_ROW, BACK2, a, up)

    def all_of(slots_pieces):
        def step(col):
            for slot, piece in slots_pieces:
                arrive(col, slot, piece)

        by_column(step)

    def mm(x, w):
        return jnp.dot(x, w, preferred_element_type=jnp.float32)

    load_h.wait()
    load_k0.wait()
    kv_sum[:, 0:256] = mm(h_own[...], wk[0])
    load_v0.wait()
    kv_sum[:, 256:512] = mm(h_own[...], wv[0])
    load_q0.wait()

    def q_own(n, _):
        cols = pl.ds(pl.multiple_of(n * 256, 256), 256)
        q_sum[:, cols] = mm(h_own[...], wq[0, :, cols])
        return 0

    lax.fori_loop(0, 4, q_own, 0)

    for blk in range(2):
        swaps[blk].wait_recv()
        if blk == 0:
            load_k1.wait()
            load_v1.wait()
        rows = slice(blk * BLK, (blk + 1) * BLK)
        keys = kv_sum[rows, 0:256] + mm(h_oth[rows], wk[1])
        values = kv_sum[rows, 256:512] + mm(h_oth[rows], wv[1])
        for g in range(2):
            cols = slice(g * HEAD, (g + 1) * HEAD)
            kv[OWN, 2 * blk + g, 0:128] = keys[:, cols].astype(jnp.bfloat16)
            kv[OWN, 2 * blk + g, 128:256] = values[:, cols].T.astype(jnp.bfloat16)
        by_column(send_first if blk == 0 else send_second)

    load_q1.wait()

    def q_oth(n, _):
        cols = pl.ds(pl.multiple_of(n * 256, 256), 256)
        q = (q_sum[:, cols] + mm(h_oth[...], wq[1, :, cols])).astype(jnp.bfloat16)
        g, pair = n // 2, lax.rem(n, 2)
        for blk in range(2):
            for j in range(2):
                first = pl.multiple_of((blk * 4 + pair * 2 + j) * BLK, BLK)
                qs[g, pl.ds(first, BLK)] = q[blk * BLK : (blk + 1) * BLK, j * HEAD : (j + 1) * HEAD]
        return 0

    lax.fori_loop(0, 4, q_oth, 0)

    factor = math.log2(math.e) / math.sqrt(HEAD)

    def update(g, chunk, blocks, causal=False, first=False, last=False):
        lanes = pl.ds(pl.multiple_of(chunk * 256, 256), 256)
        q = qs[g, lanes]
        low = low_row[0:1, lanes]
        scores = []
        for slot, blk, back in blocks:
            s = lax.dot_general(
                kv[slot, 2 * blk + g, 0:128], q, NT, preferred_element_type=jnp.float32
            )
            k_pos = ((here - back) * 2 + blk) * BLK + lax.broadcasted_iota(
                jnp.int32, (BLK, 256), 0
            )
            allowed = k_pos >= low
            if causal:
                allowed = allowed & (k_pos <= pos_row[0:1, lanes])
            scores.append(jnp.where(allowed, s * factor, NEG))
        top = functools.reduce(jnp.maximum, [jnp.max(s, axis=0, keepdims=True) for s in scores])
        if not first:
            old = m_s[g, 0:1, lanes]
            top = jnp.maximum(old, top)
            shrink = jnp.exp2(old - top)
        parts = [jnp.exp2(s - top) for s in scores]
        total = sum(jnp.sum(p.reshape(BLK // 8, 8, 256), axis=0) for p in parts)
        weights = jnp.concatenate([p.astype(jnp.bfloat16) for p in parts], axis=0)
        values = jnp.concatenate([kv[slot, 2 * blk + g, 128:256] for slot, blk, _ in blocks], axis=1)
        mixed = mm(values, weights)
        if not first:
            total = total + l_s[g, :, lanes] * shrink
            mixed = mixed + acc_s[g, :, lanes] * shrink
        if not last:
            m_s[g, 0:1, lanes] = top
            l_s[g, :, lanes] = total
            acc_s[g, :, lanes] = mixed
            return
        mixed = mixed / jnp.sum(total, axis=0, keepdims=True)
        blk, pair = chunk // 2, lax.rem(chunk, 2)
        rows = pl.ds(pl.multiple_of(blk * BLK, BLK), BLK)
        for j in range(2):
            cols = pl.ds(pl.multiple_of((g * 4 + pair * 2 + j) * HEAD, HEAD), HEAD)
            out[rows, cols] = mixed[:, j * HEAD : (j + 1) * HEAD].T.astype(jnp.bfloat16)

    def sweep(g, chunks, blocks, **how):
        def step(chunk, _):
            update(g, chunk, blocks, **how)
            return 0

        lax.fori_loop(chunks[0], chunks[1], step, 0)

    for g in range(2):
        sweep(g, (0, 2), [(OWN, 0, 0)], causal=True, first=True)
        sweep(g, (2, 4), [(OWN, 0, 0), (OWN, 1, 0)], causal=True, first=True)

    for step in (relay_first, relay_second, relay_third):
        for i in range(2):
            by_column(functools.partial(step, i))

    for g in range(2):
        all_of([(BACK1, g), (BACK1, 2 + g)])
        sweep(g, (0, 4), [(BACK1, 0, 1), (BACK1, 1, 1)])
    for g in range(2):
        all_of([(BACK3, g), (BACK3, 2 + g), (BACK4, 2 + g)])
        sweep(g, (0, 2), [(BACK4, 1, 4), (BACK3, 0, 3), (BACK3, 1, 3)])
        sweep(g, (2, 4), [(BACK3, 1, 3)])
    for g in range(2):
        all_of([(BACK2, g), (BACK2, 2 + g)])
        sweep(g, (0, 4), [(BACK2, 0, 2), (BACK2, 1, 2)], last=True)

    for swap in swaps:
        swap.wait_send()

    def finish(col):
        for k in range(sends[col]):
            copy(OWN, BACK1, 0, up, k).wait_send()

    by_column(finish)


def local(hidden, block_owner, doc_lengths, w_query, w_key, value_weight):
    rows, half = hidden.shape
    q_cols, k_cols = w_query.shape[1], w_key.shape[1]
    groups = k_cols // HEAD
    shards = lax.axis_size("ctx")
    bf16, f32 = jnp.bfloat16, jnp.float32
    lanes = rows * q_cols // k_cols
    dma = pltpu.SemaphoreType.DMA
    any_spec = pl.BlockSpec(memory_space=pl.ANY)
    smem_spec = pl.BlockSpec(memory_space=pltpu.SMEM)
    macs = rows * 2 * half * (q_cols + 2 * k_cols)
    return pl.pallas_call(
        functools.partial(kernel, shards),
        out_shape=jax.ShapeDtypeStruct((rows, q_cols), bf16),
        in_specs=[any_spec, smem_spec, smem_spec, any_spec, any_spec, any_spec],
        out_specs=pl.BlockSpec(memory_space=pltpu.VMEM),
        scratch_shapes=[
            pltpu.VMEM((rows, half), bf16),
            pltpu.VMEM((rows, half), bf16),
            pltpu.VMEM((2, half, q_cols), bf16),
            pltpu.VMEM((2, half, k_cols), bf16),
            pltpu.VMEM((2, half, k_cols), bf16),
            pltpu.VMEM((rows, 2 * k_cols), f32),
            pltpu.VMEM((rows, q_cols), f32),
            pltpu.VMEM((groups, lanes, HEAD), bf16),
            pltpu.VMEM((8, 4, 2 * BLK, HEAD), bf16),
            pltpu.VMEM((8, lanes), jnp.int32),
            pltpu.VMEM((8, lanes), jnp.int32),
            pltpu.VMEM((groups, 8, lanes), f32),
            pltpu.VMEM((groups, 8, lanes), f32),
            pltpu.VMEM((groups, HEAD, lanes), f32),
            dma((7,)),
            dma((2,)),
            dma((2,)),
            dma((20,)),
            dma((8, 4)),
        ],
        compiler_params=pltpu.CompilerParams(
            collective_id=0, has_side_effects=True, vmem_limit_bytes=56 << 20
        ),
        cost_estimate=pl.CostEstimate(
            flops=4 * macs, bytes_accessed=16 << 20, transcendentals=2 << 20
        ),
        name="attention",
    )(hidden, block_owner, doc_lengths, w_query, w_key, value_weight)


def solution(mesh):
    in_specs = (P("ctx", "head"), P(), P(), P(None, "head"), P(None, "head"), P(None, "head"))
    out_specs = P("ctx", "head")
    return jax.shard_map(local, mesh=mesh, in_specs=in_specs, out_specs=out_specs, check_vma=False)
```

```python
import functools
import math

import jax
import jax.numpy as jnp
from jax import lax
from jax.experimental import pallas as pl
from jax.experimental.pallas import tpu as pltpu
from jax.sharding import PartitionSpec as P

HEAD = 128
BLK = 128
REACH = 2
NEG = -1e30
MESH = pl.DeviceIdType.MESH
OWN, BACK1, BACK3, BACK2, BACK4, PASS_UP, PASS_DOWN, PASS_ROW = range(8)


def kernel(
    shards,
    hid,
    owner,
    lengths,
    w_q,
    w_k,
    w_v,
    out,
    h_own,
    h_oth,
    wq,
    wk,
    wv,
    kv_sum,
    q_sum,
    qs,
    kv,
    low_row,
    pos_row,
    m_s,
    l_s,
    acc_s,
    s_buf,
    p_buf,
    shrink_s,
    load_sem,
    hid_send,
    hid_recv,
    send_sem,
    recv_sem,
):
    here = lax.axis_index("ctx")
    head = lax.axis_index("head")
    z = lax.rem(here, 4)
    ring = here - z
    up = ring + lax.rem(z + 1, 4)
    down = ring + lax.rem(z + 3, 4)
    row_next = lax.rem(here + 4, shards)
    row_prev = lax.rem(here + shards - 4, shards)
    half = h_own.shape[1]
    mine = pl.multiple_of(head * half, half)
    other = pl.multiple_of((1 - head) * half, half)

    loads = [pltpu.make_async_copy(hid, h_own, load_sem.at[0])]
    for part, first in ((0, mine), (1, other)):
        for src, dst in ((w_k, wk), (w_v, wv)):
            loads.append(
                pltpu.make_async_copy(
                    src.at[pl.ds(first, half)], dst.at[part], load_sem.at[len(loads)]
                )
            )
    for part, first in ((0, mine), (1, other)):
        loads.append(
            pltpu.make_async_copy(
                w_q.at[pl.ds(first, half)], wq.at[part], load_sem.at[len(loads)]
            )
        )
    for load in loads:
        load.start()
    load_h, load_k0, load_v0, load_k1, load_v1, load_q0, load_q1 = loads

    @pl.when(here < 4)
    def _():
        for slot in (BACK1, BACK3, BACK2, BACK4):
            kv[slot] = jnp.zeros(kv.shape[1:], kv.dtype)

    barrier = pltpu.get_barrier_semaphore()
    for peer in ((here, 1 - head), (up, head), (down, head), (row_prev, head)):
        pl.semaphore_signal(barrier, inc=1, device_id=peer, device_id_type=MESH)
    pl.semaphore_wait(barrier, 4)

    swaps = []
    for blk in range(2):
        rows = pl.ds(blk * BLK, BLK)
        swaps.append(
            pltpu.make_async_remote_copy(
                src_ref=hid.at[rows],
                dst_ref=h_oth.at[rows],
                send_sem=hid_send.at[blk],
                recv_sem=hid_recv.at[blk],
                device_id=(here, 1 - head),
                device_id_type=MESH,
            )
        )
        swaps[-1].start()

    first_block = 2 * here - 8
    lane = lax.broadcasted_iota(jnp.int32, (8, BLK), 1)
    for blk in range(2):
        shard = owner[2 * here + blk]
        low = jnp.maximum(first_block, 0)
        for j in range(10):
            block = first_block + j
            below = owner[jnp.maximum(block, 0)] < shard - REACH
            low = low + jnp.where(below & (block >= 0), 1, 0)
        pos = (2 * here + blk) * BLK + lane
        start = jnp.int32(0)
        doc = jnp.zeros((8, BLK), jnp.int32)
        for i in range(lengths.shape[0]):
            doc = jnp.where(pos >= start, start, doc)
            start = start + lengths[i]
        lower = jnp.maximum(doc, low * BLK)
        for hh in range(4):
            cols = slice((blk * 4 + hh) * BLK, (blk * 4 + hh + 1) * BLK)
            low_row[:, cols] = lower
            pos_row[:, cols] = pos

    def copy(src, dst, piece, to, k):
        return pltpu.make_async_remote_copy(
            src_ref=kv.at[src, piece],
            dst_ref=kv.at[dst, piece],
            send_sem=send_sem.at[k],
            recv_sem=recv_sem.at[dst, piece],
            device_id=(to, head),
            device_id_type=MESH,
        )

    first_row, last_row = here < 4, here >= shards - 4
    sends = [[0] * 3 for _ in range(4)]
    waited = [set(), set(), set(), set()]

    ALWAYS, CROSS, LATER = range(3)

    def guarded(kind, action):
        if kind == ALWAYS:
            action()
        else:
            pl.when(jnp.logical_not(last_row if kind == CROSS else first_row))(action)

    def send(col, src, dst, piece, to, kind=ALWAYS):
        k = 8 * kind + sends[col][kind]
        sends[col][kind] += 1
        guarded(kind, lambda: copy(src, dst, piece, to, k).start())

    def from_row_before(col, slot):
        return (
            slot in (BACK4, PASS_ROW)
            or (slot == BACK1 and col == 0)
            or (slot == BACK3 and col < 3)
            or (slot == BACK2 and col < 2)
        )

    def arrive(col, slot, piece):
        if (slot, piece) not in waited[col]:
            waited[col].add((slot, piece))
            guarded(
                LATER if from_row_before(col, slot) else ALWAYS,
                lambda: copy(OWN, slot, piece, up, 0).wait_recv(),
            )

    def by_column(step):
        for col in range(4):
            pl.when(z == col)(functools.partial(step, col))

    A, B = (0, 1), (2, 3)

    def send_first(col):
        for a in A:
            send(col, OWN, BACK1 if col < 3 else PASS_UP, a, up)
            send(col, OWN, PASS_DOWN if col > 0 else BACK3, a, down)

    def send_second(col):
        for b in B:
            send(col, OWN, BACK4, b, row_next, CROSS)
            if col < 3:
                send(col, OWN, BACK1, b, up)
            if col == 0:
                send(col, OWN, BACK3, b, down)

    def relay_first(i, col):
        a, b = A[i], B[i]
        if col == 0:
            arrive(col, PASS_DOWN, a)
            send(col, PASS_DOWN, BACK3, a, row_next, CROSS)
            send(col, PASS_DOWN, BACK2, a, down)
            arrive(col, PASS_UP, a)
            send(col, PASS_UP, BACK1, a, row_next, CROSS)
        if col in (1, 2):
            arrive(col, PASS_DOWN, a)
            send(col, PASS_DOWN, BACK3, a, row_next, CROSS)
        if col == 1:
            arrive(col, BACK1, a)
            send(col, BACK1, BACK2, a, up)
        if col == 3:
            arrive(col, BACK1, a)
            send(col, BACK1, PASS_ROW, a, row_next, CROSS)
        if col > 0:
            arrive(col, BACK4, b)
            send(col, BACK4, BACK3, b, down, LATER)
        if col == 3:
            send(col, BACK4, BACK1, b, up, LATER)

    def relay_second(i, col):
        b = B[i]
        if col == 2:
            arrive(col, BACK1, b)
            send(col, BACK1, BACK2, b, up)
        if col == 3:
            arrive(col, BACK3, b)
            send(col, BACK3, BACK2, b, down)

    def relay_third(i, col):
        a, b = A[i], B[i]
        if col == 0:
            arrive(col, BACK1, b)
            send(col, BACK1, BACK2, b, up, LATER)
        if col == 1:
            arrive(col, BACK3, b)
            send(col, BACK3, BACK2, b, down, LATER)
        if col == 2:
            arrive(col, BACK3, a)
            send(col, BACK3, BACK2, a, down, LATER)
        if col == 3:
            arrive(col, PASS_ROW, a)
            send(col, PASS_ROW, BACK2, a, up, LATER)

    def all_of(slots_pieces):
        def step(col):
            for slot, piece in slots_pieces:
                arrive(col, slot, piece)

        by_column(step)

    def mm(x, w):
        return jnp.dot(x, w, preferred_element_type=jnp.float32)

    load_h.wait()
    load_k0.wait()
    kv_sum[:, 0:256] = mm(h_own[...], wk[0])
    load_v0.wait()
    kv_sum[:, 256:512] = mm(h_own[...], wv[0])
    load_q0.wait()

    def q_own(n, _):
        cols = pl.ds(pl.multiple_of(n * 256, 256), 256)
        q_sum[:, cols] = mm(h_own[...], wq[0, :, cols])
        return 0

    lax.fori_loop(0, 4, q_own, 0)

    for blk in range(2):
        swaps[blk].wait_recv()
        if blk == 0:
            load_k1.wait()
            load_v1.wait()
        rows = slice(blk * BLK, (blk + 1) * BLK)
        keys = kv_sum[rows, 0:256] + mm(h_oth[rows], wk[1])
        values = kv_sum[rows, 256:512] + mm(h_oth[rows], wv[1])
        for g in range(2):
            cols = slice(g * HEAD, (g + 1) * HEAD)
            kv[OWN, 2 * blk + g, 0:128] = keys[:, cols].astype(jnp.bfloat16)
            kv[OWN, 2 * blk + g, 128:256] = values[:, cols].T.astype(jnp.bfloat16)
        by_column(send_first if blk == 0 else send_second)

    load_q1.wait()

    def q_oth(n, _):
        cols = pl.ds(pl.multiple_of(n * 256, 256), 256)
        q = (q_sum[:, cols] + mm(h_oth[...], wq[1, :, cols])).astype(jnp.bfloat16)
        g, pair = n // 2, lax.rem(n, 2)
        for blk in range(2):
            for j in range(2):
                first = pl.multiple_of((blk * 4 + pair * 2 + j) * BLK, BLK)
                qs[g, :, pl.ds(first, BLK)] = q[blk * BLK : (blk + 1) * BLK, j * HEAD : (j + 1) * HEAD].T
        return 0

    lax.fori_loop(0, 4, q_oth, 0)

    factor = math.log2(math.e) / math.sqrt(HEAD)

    def scores_of(slot, g, chunk, blocks, causal, first, last):
        q = qs[g, :, chunk * 256 : (chunk + 1) * 256]
        for i, (src, blk, _) in enumerate(blocks):
            s_buf[slot, i * BLK : (i + 1) * BLK] = mm(kv[src, 2 * blk + g, 0:128], q)

    def weights_of(slot, g, chunk, blocks, causal, first, last):
        lanes = slice(chunk * 256, (chunk + 1) * 256)
        low = low_row[0:1, lanes]
        parts = []
        for i, (_, blk, back) in enumerate(blocks):
            k_pos = ((here - back) * 2 + blk) * BLK + lax.broadcasted_iota(
                jnp.int32, (BLK, 256), 0
            )
            allowed = k_pos >= low
            if causal:
                allowed = allowed & (k_pos <= pos_row[0:1, lanes])
            parts.append(jnp.where(allowed, s_buf[slot, i * BLK : (i + 1) * BLK] * factor, NEG))
        top = functools.reduce(jnp.maximum, [p.reshape(BLK // 8, 8, 256).max(axis=0) for p in parts])
        top = jnp.max(top, axis=0, keepdims=True)
        if not first:
            old = m_s[g, 0:1, lanes]
            top = jnp.maximum(old, top)
            shrink = jnp.exp2(old - top)
            shrink_s[slot, 0:1] = shrink
        if not last:
            m_s[g, 0:1, lanes] = top
        total = None
        for i, s in enumerate(parts):
            p = jnp.exp2(s - top)
            p_buf[slot, i * BLK : (i + 1) * BLK] = p.astype(jnp.bfloat16)
            p = p.reshape(BLK // 8, 8, 256).sum(axis=0)
            total = p if total is None else total + p
        l_s[g, :, lanes] = total if first else total + l_s[g, :, lanes] * shrink

    def mix_of(slot, g, chunk, blocks, causal, first, last):
        lanes = slice(chunk * 256, (chunk + 1) * 256)
        values = jnp.concatenate([kv[src, 2 * blk + g, 128:256] for src, blk, _ in blocks], axis=1)
        mixed = mm(values, p_buf[slot, 0 : len(blocks) * BLK])
        if not first:
            mixed = mixed + acc_s[g, :, lanes] * shrink_s[slot, 0:1]
        if not last:
            acc_s[g, :, lanes] = mixed
            return
        mixed = mixed / jnp.sum(l_s[g, :, lanes], axis=0, keepdims=True)
        rows = slice(chunk // 2 * BLK, (chunk // 2 + 1) * BLK)
        for j in range(2):
            at = g * 4 + chunk % 2 * 2 + j
            out[rows, at * HEAD : (at + 1) * HEAD] = (
                mixed[:, j * HEAD : (j + 1) * HEAD].T.astype(jnp.bfloat16)
            )

    def run(tasks):
        count = len(tasks)
        for i in range(count + 2):
            for stage, j in ((scores_of, i), (mix_of, i - 2), (weights_of, i - 1)):
                if 0 <= j < count:
                    stage(j % 3, *tasks[j])

    def task(g, chunk, blocks, causal=False, first=False, last=False):
        return g, chunk, blocks, causal, first, last

    own = [(OWN, 0, 0), (OWN, 1, 0)]
    run(
        [
            task(g, chunk, own[: 1 + chunk // 2], causal=True, first=True)
            for g in range(2)
            for chunk in range(4)
        ]
    )

    for step in (relay_first, relay_second, relay_third):
        for i in range(2):
            by_column(functools.partial(step, i))

    all_of([(BACK1, piece) for piece in range(4)])
    back1 = [(BACK1, 0, 1), (BACK1, 1, 1)]
    run([task(g, chunk, back1) for g in range(2) for chunk in range(4)])
    all_of([(BACK3, piece) for piece in range(4)] + [(BACK4, b) for b in B])
    back3 = [(BACK4, 1, 4), (BACK3, 0, 3), (BACK3, 1, 3)]
    run([task(g, chunk, back3[chunk // 2 * 2 :]) for g in range(2) for chunk in range(4)])
    back2 = [(BACK2, 0, 2), (BACK2, 1, 2)]
    for g in range(2):
        all_of([(BACK2, g), (BACK2, 2 + g)])
        run([task(g, chunk, back2, last=True) for chunk in range(4)])

    for swap in swaps:
        swap.wait_send()

    def finish(col):
        for kind in range(3):
            for k in range(sends[col][kind]):
                guarded(kind, lambda k=8 * kind + k: copy(OWN, BACK1, 0, up, k).wait_send())

    by_column(finish)


def local(hidden, block_owner, doc_lengths, w_query, w_key, value_weight):
    rows, half = hidden.shape
    q_cols, k_cols = w_query.shape[1], w_key.shape[1]
    groups = k_cols // HEAD
    shards = lax.axis_size("ctx")
    bf16, f32 = jnp.bfloat16, jnp.float32
    lanes = rows * q_cols // k_cols
    dma = pltpu.SemaphoreType.DMA
    any_spec = pl.BlockSpec(memory_space=pl.ANY)
    smem_spec = pl.BlockSpec(memory_space=pltpu.SMEM)
    macs = rows * 2 * half * (q_cols + 2 * k_cols)
    return pl.pallas_call(
        functools.partial(kernel, shards),
        out_shape=jax.ShapeDtypeStruct((rows, q_cols), bf16),
        in_specs=[any_spec, smem_spec, smem_spec, any_spec, any_spec, any_spec],
        out_specs=pl.BlockSpec(memory_space=pltpu.VMEM),
        scratch_shapes=[
            pltpu.VMEM((rows, half), bf16),
            pltpu.VMEM((rows, half), bf16),
            pltpu.VMEM((2, half, q_cols), bf16),
            pltpu.VMEM((2, half, k_cols), bf16),
            pltpu.VMEM((2, half, k_cols), bf16),
            pltpu.VMEM((rows, 2 * k_cols), f32),
            pltpu.VMEM((rows, q_cols), f32),
            pltpu.VMEM((groups, HEAD, lanes), bf16),
            pltpu.VMEM((8, 4, 2 * BLK, HEAD), bf16),
            pltpu.VMEM((8, lanes), jnp.int32),
            pltpu.VMEM((8, lanes), jnp.int32),
            pltpu.VMEM((groups, 8, lanes), f32),
            pltpu.VMEM((groups, 8, lanes), f32),
            pltpu.VMEM((groups, HEAD, lanes), f32),
            pltpu.VMEM((3, 3 * BLK, 256), f32),
            pltpu.VMEM((3, 3 * BLK, 256), bf16),
            pltpu.VMEM((3, 8, 256), f32),
            dma((7,)),
            dma((2,)),
            dma((2,)),
            dma((24,)),
            dma((8, 4)),
        ],
        compiler_params=pltpu.CompilerParams(
            collective_id=0, has_side_effects=True, vmem_limit_bytes=56 << 20
        ),
        cost_estimate=pl.CostEstimate(
            flops=4 * macs, bytes_accessed=16 << 20, transcendentals=2 << 20
        ),
        name="attention",
    )(hidden, block_owner, doc_lengths, w_query, w_key, value_weight)


def solution(mesh):
    in_specs = (P("ctx", "head"), P(), P(), P(None, "head"), P(None, "head"), P(None, "head"))
    out_specs = P("ctx", "head")
    return jax.shard_map(local, mesh=mesh, in_specs=in_specs, out_specs=out_specs, check_vma=False)
```

```python
import functools
import math

import jax
import jax.numpy as jnp
from jax import lax
from jax.experimental import pallas as pl
from jax.experimental.pallas import tpu as pltpu
from jax.sharding import PartitionSpec as P

HEAD = 128
BLK = 128
REACH = 2
NEG = -1e30
MESH = pl.DeviceIdType.MESH
OWN, BACK1, BACK3, BACK2, BACK4, PASS_UP, PASS_DOWN, PASS_ROW = range(8)


def kernel(
    shards,
    hid,
    owner_hbm,
    lengths_hbm,
    w_q,
    w_k,
    w_v,
    out,
    owner,
    lengths,
    h_own,
    h_oth,
    wq,
    wk,
    wv,
    kv_sum,
    q_sum,
    qs,
    kv,
    low_row,
    pos_row,
    m_s,
    l_s,
    acc_s,
    s_buf,
    p_buf,
    shrink_s,
    load_sem,
    hid_send,
    hid_recv,
    send_sem,
    recv_sem,
):
    here = lax.axis_index("ctx")
    head = lax.axis_index("head")
    z = lax.rem(here, 4)
    ring = here - z
    up = ring + lax.rem(z + 1, 4)
    down = ring + lax.rem(z + 3, 4)
    row_next = lax.rem(here + 4, shards)
    row_prev = lax.rem(here + shards - 4, shards)
    half = h_own.shape[1]
    mine = pl.multiple_of(head * half, half)
    other = pl.multiple_of((1 - head) * half, half)

    loads = [pltpu.make_async_copy(hid, h_own, load_sem.at[0])]
    for part, first in ((0, mine), (1, other)):
        for src, dst in ((w_k, wk), (w_v, wv)):
            loads.append(
                pltpu.make_async_copy(
                    src.at[pl.ds(first, half)], dst.at[part], load_sem.at[len(loads)]
                )
            )
    for part, first in ((0, mine), (1, other)):
        loads.append(
            pltpu.make_async_copy(
                w_q.at[pl.ds(first, half)], wq.at[part], load_sem.at[len(loads)]
            )
        )
    tables = [
        pltpu.make_async_copy(owner_hbm, owner, load_sem.at[7]),
        pltpu.make_async_copy(lengths_hbm, lengths, load_sem.at[8]),
    ]
    for load in tables + loads:
        load.start()
    load_h, load_k0, load_v0, load_k1, load_v1, load_q0, load_q1 = loads

    @pl.when(here < 4)
    def _():
        for slot in (BACK1, BACK3, BACK2, BACK4):
            kv[slot] = jnp.zeros(kv.shape[1:], kv.dtype)

    barrier = pltpu.get_barrier_semaphore()
    for peer in ((here, 1 - head), (up, head), (down, head), (row_prev, head)):
        pl.semaphore_signal(barrier, inc=1, device_id=peer, device_id_type=MESH)
    pl.semaphore_wait(barrier, 4)

    swaps = []
    for blk in range(2):
        rows = pl.ds(blk * BLK, BLK)
        swaps.append(
            pltpu.make_async_remote_copy(
                src_ref=hid.at[rows],
                dst_ref=h_oth.at[rows],
                send_sem=hid_send.at[blk],
                recv_sem=hid_recv.at[blk],
                device_id=(here, 1 - head),
                device_id_type=MESH,
            )
        )
        swaps[-1].start()

    for table in tables:
        table.wait()
    first_block = 2 * here - 8
    lane = lax.broadcasted_iota(jnp.int32, (8, BLK), 1)
    for blk in range(2):
        shard = owner[2 * here + blk]
        low = jnp.maximum(first_block, 0)
        for j in range(10):
            block = first_block + j
            below = owner[jnp.maximum(block, 0)] < shard - REACH
            low = low + jnp.where(below & (block >= 0), 1, 0)
        pos = (2 * here + blk) * BLK + lane
        start = jnp.int32(0)
        doc = jnp.zeros((8, BLK), jnp.int32)
        for i in range(lengths.shape[0]):
            doc = jnp.where(pos >= start, start, doc)
            start = start + lengths[i]
        lower = jnp.maximum(doc, low * BLK)
        for hh in range(4):
            cols = slice((blk * 4 + hh) * BLK, (blk * 4 + hh + 1) * BLK)
            low_row[:, cols] = lower
            pos_row[:, cols] = pos

    def copy(src, dst, piece, to, k):
        return pltpu.make_async_remote_copy(
            src_ref=kv.at[src, piece],
            dst_ref=kv.at[dst, piece],
            send_sem=send_sem.at[k],
            recv_sem=recv_sem.at[dst, piece],
            device_id=(to, head),
            device_id_type=MESH,
        )

    first_row, last_row = here < 4, here >= shards - 4
    sends = [[0] * 3 for _ in range(4)]
    waited = [set(), set(), set(), set()]

    ALWAYS, CROSS, LATER = range(3)

    def guarded(kind, action):
        if kind == ALWAYS:
            action()
        else:
            pl.when(jnp.logical_not(last_row if kind == CROSS else first_row))(action)

    def send(col, src, dst, piece, to, kind=ALWAYS):
        k = 8 * kind + sends[col][kind]
        sends[col][kind] += 1
        guarded(kind, lambda: copy(src, dst, piece, to, k).start())

    def from_row_before(col, slot):
        return (
            slot in (BACK4, PASS_ROW)
            or (slot == BACK1 and col == 0)
            or (slot == BACK3 and col < 3)
            or (slot == BACK2 and col < 2)
        )

    def arrive(col, slot, piece):
        if (slot, piece) not in waited[col]:
            waited[col].add((slot, piece))
            guarded(
                LATER if from_row_before(col, slot) else ALWAYS,
                lambda: copy(OWN, slot, piece, up, 0).wait_recv(),
            )

    def by_column(step):
        for col in range(4):
            pl.when(z == col)(functools.partial(step, col))

    A, B = (0, 1), (2, 3)

    def send_first(col):
        for a in A:
            send(col, OWN, BACK1 if col < 3 else PASS_UP, a, up)
            send(col, OWN, PASS_DOWN if col > 0 else BACK3, a, down)

    def send_second(col):
        for b in B:
            send(col, OWN, BACK4, b, row_next, CROSS)
            if col < 3:
                send(col, OWN, BACK1, b, up)
            if col == 0:
                send(col, OWN, BACK3, b, down)

    def relay_first(i, col):
        a, b = A[i], B[i]
        if col == 0:
            arrive(col, PASS_DOWN, a)
            send(col, PASS_DOWN, BACK3, a, row_next, CROSS)
            send(col, PASS_DOWN, BACK2, a, down)
            arrive(col, PASS_UP, a)
            send(col, PASS_UP, BACK1, a, row_next, CROSS)
        if col in (1, 2):
            arrive(col, PASS_DOWN, a)
            send(col, PASS_DOWN, BACK3, a, row_next, CROSS)
        if col == 1:
            arrive(col, BACK1, a)
            send(col, BACK1, BACK2, a, up)
        if col == 3:
            arrive(col, BACK1, a)
            send(col, BACK1, PASS_ROW, a, row_next, CROSS)
        if col > 0:
            arrive(col, BACK4, b)
            send(col, BACK4, BACK3, b, down, LATER)
        if col == 3:
            send(col, BACK4, BACK1, b, up, LATER)

    def relay_second(i, col):
        b = B[i]
        if col == 2:
            arrive(col, BACK1, b)
            send(col, BACK1, BACK2, b, up)
        if col == 3:
            arrive(col, BACK3, b)
            send(col, BACK3, BACK2, b, down)

    def relay_third(i, col):
        a, b = A[i], B[i]
        if col == 0:
            arrive(col, BACK1, b)
            send(col, BACK1, BACK2, b, up, LATER)
        if col == 1:
            arrive(col, BACK3, b)
            send(col, BACK3, BACK2, b, down, LATER)
        if col == 2:
            arrive(col, BACK3, a)
            send(col, BACK3, BACK2, a, down, LATER)
        if col == 3:
            arrive(col, PASS_ROW, a)
            send(col, PASS_ROW, BACK2, a, up, LATER)

    def all_of(slots_pieces):
        def step(col):
            for slot, piece in slots_pieces:
                arrive(col, slot, piece)

        by_column(step)

    def mm(x, w):
        return jnp.dot(x, w, preferred_element_type=jnp.float32)

    load_h.wait()
    load_k0.wait()
    kv_sum[:, 0:256] = mm(h_own[...], wk[0])
    load_v0.wait()
    kv_sum[:, 256:512] = mm(h_own[...], wv[0])
    load_q0.wait()

    def q_own(n, _):
        cols = pl.ds(pl.multiple_of(n * 256, 256), 256)
        q_sum[:, cols] = mm(h_own[...], wq[0, :, cols])
        return 0

    lax.fori_loop(0, 4, q_own, 0)

    for blk in range(2):
        swaps[blk].wait_recv()
        if blk == 0:
            load_k1.wait()
            load_v1.wait()
        rows = slice(blk * BLK, (blk + 1) * BLK)
        keys = kv_sum[rows, 0:256] + mm(h_oth[rows], wk[1])
        values = kv_sum[rows, 256:512] + mm(h_oth[rows], wv[1])
        for g in range(2):
            cols = slice(g * HEAD, (g + 1) * HEAD)
            kv[OWN, 2 * blk + g, 0:128] = keys[:, cols].astype(jnp.bfloat16)
            kv[OWN, 2 * blk + g, 128:256] = values[:, cols].T.astype(jnp.bfloat16)
        by_column(send_first if blk == 0 else send_second)

    load_q1.wait()

    def q_oth(n, _):
        cols = pl.ds(pl.multiple_of(n * 256, 256), 256)
        q = (q_sum[:, cols] + mm(h_oth[...], wq[1, :, cols])).astype(jnp.bfloat16)
        g, pair = n // 2, lax.rem(n, 2)
        for blk in range(2):
            for j in range(2):
                first = pl.multiple_of((blk * 4 + pair * 2 + j) * BLK, BLK)
                qs[g, :, pl.ds(first, BLK)] = q[blk * BLK : (blk + 1) * BLK, j * HEAD : (j + 1) * HEAD].T
        return 0

    lax.fori_loop(0, 4, q_oth, 0)

    factor = math.log2(math.e) / math.sqrt(HEAD)

    def scores_of(slot, g, chunk, blocks, causal, first, last):
        q = qs[g, :, chunk * 256 : (chunk + 1) * 256]
        for i, (src, blk, _) in enumerate(blocks):
            s_buf[slot, i * BLK : (i + 1) * BLK] = mm(kv[src, 2 * blk + g, 0:128], q)

    def weights_of(slot, g, chunk, blocks, causal, first, last):
        lanes = slice(chunk * 256, (chunk + 1) * 256)
        low = low_row[0:1, lanes]
        parts = []
        for i, (_, blk, back) in enumerate(blocks):
            k_pos = ((here - back) * 2 + blk) * BLK + lax.broadcasted_iota(
                jnp.int32, (BLK, 256), 0
            )
            allowed = k_pos >= low
            if causal:
                allowed = allowed & (k_pos <= pos_row[0:1, lanes])
            parts.append(jnp.where(allowed, s_buf[slot, i * BLK : (i + 1) * BLK] * factor, NEG))
        top = functools.reduce(jnp.maximum, [p.reshape(BLK // 8, 8, 256).max(axis=0) for p in parts])
        top = jnp.max(top, axis=0, keepdims=True)
        if not first:
            old = m_s[g, 0:1, lanes]
            top = jnp.maximum(old, top)
            shrink = jnp.exp2(old - top)
            shrink_s[slot, 0:1] = shrink
        if not last:
            m_s[g, 0:1, lanes] = top
        total = None
        for i, s in enumerate(parts):
            p = jnp.exp2(s - top)
            p_buf[slot, i * BLK : (i + 1) * BLK] = p.astype(jnp.bfloat16)
            p = p.reshape(BLK // 8, 8, 256).sum(axis=0)
            total = p if total is None else total + p
        l_s[g, :, lanes] = total if first else total + l_s[g, :, lanes] * shrink

    def mix_of(slot, g, chunk, blocks, causal, first, last):
        lanes = slice(chunk * 256, (chunk + 1) * 256)
        values = jnp.concatenate([kv[src, 2 * blk + g, 128:256] for src, blk, _ in blocks], axis=1)
        mixed = mm(values, p_buf[slot, 0 : len(blocks) * BLK])
        if not first:
            mixed = mixed + acc_s[g, :, lanes] * shrink_s[slot, 0:1]
        if not last:
            acc_s[g, :, lanes] = mixed
            return
        mixed = mixed / jnp.sum(l_s[g, :, lanes], axis=0, keepdims=True)
        rows = slice(chunk // 2 * BLK, (chunk // 2 + 1) * BLK)
        for j in range(2):
            at = g * 4 + chunk % 2 * 2 + j
            out[rows, at * HEAD : (at + 1) * HEAD] = (
                mixed[:, j * HEAD : (j + 1) * HEAD].T.astype(jnp.bfloat16)
            )

    def run(tasks):
        count = len(tasks)
        for i in range(count + 2):
            for stage, j in ((scores_of, i), (mix_of, i - 2), (weights_of, i - 1)):
                if 0 <= j < count:
                    stage(j % 3, *tasks[j])

    def task(g, chunk, blocks, causal=False, first=False, last=False):
        return g, chunk, blocks, causal, first, last

    own = [(OWN, 0, 0), (OWN, 1, 0)]
    run(
        [
            task(g, chunk, own[: 1 + chunk // 2], causal=True, first=True)
            for g in range(2)
            for chunk in range(4)
        ]
    )

    for step in (relay_first, relay_second, relay_third):
        for i in range(2):
            by_column(functools.partial(step, i))

    all_of([(BACK1, piece) for piece in range(4)])
    back1 = [(BACK1, 0, 1), (BACK1, 1, 1)]
    run([task(g, chunk, back1) for g in range(2) for chunk in range(4)])
    all_of([(BACK3, piece) for piece in range(4)] + [(BACK4, b) for b in B])
    back3 = [(BACK4, 1, 4), (BACK3, 0, 3), (BACK3, 1, 3)]
    run([task(g, chunk, back3[chunk // 2 * 2 :]) for g in range(2) for chunk in range(4)])
    back2 = [(BACK2, 0, 2), (BACK2, 1, 2)]
    for g in range(2):
        all_of([(BACK2, g), (BACK2, 2 + g)])
        run([task(g, chunk, back2, last=True) for chunk in range(4)])

    for swap in swaps:
        swap.wait_send()

    def finish(col):
        for kind in range(3):
            for k in range(sends[col][kind]):
                guarded(kind, lambda k=8 * kind + k: copy(OWN, BACK1, 0, up, k).wait_send())

    by_column(finish)


def local(hidden, block_owner, doc_lengths, w_query, w_key, value_weight):
    rows, half = hidden.shape
    q_cols, k_cols = w_query.shape[1], w_key.shape[1]
    groups = k_cols // HEAD
    shards = lax.axis_size("ctx")
    bf16, f32 = jnp.bfloat16, jnp.float32
    lanes = rows * q_cols // k_cols
    dma = pltpu.SemaphoreType.DMA
    any_spec = pl.BlockSpec(memory_space=pl.ANY)
    macs = rows * 2 * half * (q_cols + 2 * k_cols)
    return pl.pallas_call(
        functools.partial(kernel, shards),
        out_shape=pltpu.VMEM((rows, q_cols), bf16),
        in_specs=[any_spec] * 6,
        out_specs=pl.BlockSpec(memory_space=pltpu.VMEM),
        scratch_shapes=[
            pltpu.SMEM(block_owner.shape, jnp.int32),
            pltpu.SMEM(doc_lengths.shape, jnp.int32),
            pltpu.VMEM((rows, half), bf16),
            pltpu.VMEM((rows, half), bf16),
            pltpu.VMEM((2, half, q_cols), bf16),
            pltpu.VMEM((2, half, k_cols), bf16),
            pltpu.VMEM((2, half, k_cols), bf16),
            pltpu.VMEM((rows, 2 * k_cols), f32),
            pltpu.VMEM((rows, q_cols), f32),
            pltpu.VMEM((groups, HEAD, lanes), bf16),
            pltpu.VMEM((8, 4, 2 * BLK, HEAD), bf16),
            pltpu.VMEM((8, lanes), jnp.int32),
            pltpu.VMEM((8, lanes), jnp.int32),
            pltpu.VMEM((groups, 8, lanes), f32),
            pltpu.VMEM((groups, 8, lanes), f32),
            pltpu.VMEM((groups, HEAD, lanes), f32),
            pltpu.VMEM((3, 3 * BLK, 256), f32),
            pltpu.VMEM((3, 3 * BLK, 256), bf16),
            pltpu.VMEM((3, 8, 256), f32),
            dma((9,)),
            dma((2,)),
            dma((2,)),
            dma((24,)),
            dma((8, 4)),
        ],
        compiler_params=pltpu.CompilerParams(
            collective_id=0, has_side_effects=True, vmem_limit_bytes=56 << 20
        ),
        cost_estimate=pl.CostEstimate(
            flops=4 * macs, bytes_accessed=16 << 20, transcendentals=2 << 20
        ),
        name="attention",
    )(hidden, block_owner, doc_lengths, w_query, w_key, value_weight)


def solution(mesh):
    in_specs = (P("ctx", "head"), P(), P(), P(None, "head"), P(None, "head"), P(None, "head"))
    out_specs = P("ctx", "head")
    return jax.shard_map(local, mesh=mesh, in_specs=in_specs, out_specs=out_specs, check_vma=False)
```

```python
import functools
import math

import jax
import jax.numpy as jnp
from jax import lax
from jax.experimental import pallas as pl
from jax.experimental.pallas import tpu as pltpu
from jax.sharding import PartitionSpec as P

HEAD = 128
BLK = 128
REACH = 2
NEG = -1e30
MESH = pl.DeviceIdType.MESH
OWN, BACK1, BACK3, BACK2, BACK4, PASS_UP, PASS_DOWN, PASS_ROW = range(8)


def kernel(
    shards,
    hid,
    owner_hbm,
    lengths_hbm,
    w_q,
    w_k,
    w_v,
    out,
    owner,
    lengths,
    h_own,
    h_oth,
    wq,
    wk,
    wv,
    kv_sum,
    q_sum,
    qs,
    kv,
    low_row,
    pos_row,
    m_s,
    l_s,
    acc_s,
    s_buf,
    p_buf,
    shrink_s,
    load_sem,
    hid_send,
    hid_recv,
    send_sem,
    recv_sem,
):
    here = lax.axis_index("ctx")
    head = lax.axis_index("head")
    z = lax.rem(here, 4)
    ring = here - z
    up = ring + lax.rem(z + 1, 4)
    down = ring + lax.rem(z + 3, 4)
    row_next = lax.rem(here + 4, shards)
    row_prev = lax.rem(here + shards - 4, shards)
    half = h_own.shape[1]
    mine = pl.multiple_of(head * half, half)
    other = pl.multiple_of((1 - head) * half, half)

    loads = [pltpu.make_async_copy(hid, h_own, load_sem.at[0])]
    for part, first in ((0, mine), (1, other)):
        for src, dst in ((w_k, wk), (w_v, wv)):
            loads.append(
                pltpu.make_async_copy(
                    src.at[pl.ds(first, half)], dst.at[part], load_sem.at[len(loads)]
                )
            )
    for part, first in ((0, mine), (1, other)):
        loads.append(
            pltpu.make_async_copy(
                w_q.at[pl.ds(first, half)], wq.at[part], load_sem.at[len(loads)]
            )
        )
    tables = [
        pltpu.make_async_copy(owner_hbm, owner, load_sem.at[7]),
        pltpu.make_async_copy(lengths_hbm, lengths, load_sem.at[8]),
    ]
    for load in tables + loads:
        load.start()
    load_h, load_k0, load_v0, load_k1, load_v1, load_q0, load_q1 = loads

    @pl.when(here < 4)
    def _():
        for slot in (BACK1, BACK3, BACK2, BACK4):
            kv[slot] = jnp.zeros(kv.shape[1:], kv.dtype)

    barrier = pltpu.get_barrier_semaphore()
    for peer in ((here, 1 - head), (up, head), (down, head), (row_prev, head)):
        pl.semaphore_signal(barrier, inc=1, device_id=peer, device_id_type=MESH)
    pl.semaphore_wait(barrier, 4)

    swaps = []
    for blk in range(2):
        rows = pl.ds(blk * BLK, BLK)
        swaps.append(
            pltpu.make_async_remote_copy(
                src_ref=hid.at[rows],
                dst_ref=h_oth.at[rows],
                send_sem=hid_send.at[blk],
                recv_sem=hid_recv.at[blk],
                device_id=(here, 1 - head),
                device_id_type=MESH,
            )
        )
        swaps[-1].start()

    for table in tables:
        table.wait()
    first_block = 2 * here - 8
    lane = lax.broadcasted_iota(jnp.int32, (8, BLK), 1)
    for blk in range(2):
        shard = owner[2 * here + blk]
        low = jnp.maximum(first_block, 0)
        for j in range(10):
            block = first_block + j
            below = owner[jnp.maximum(block, 0)] < shard - REACH
            low = low + jnp.where(below & (block >= 0), 1, 0)
        pos = (2 * here + blk) * BLK + lane
        start = jnp.int32(0)
        doc = jnp.zeros((8, BLK), jnp.int32)
        for i in range(lengths.shape[0]):
            doc = jnp.where(pos >= start, start, doc)
            start = start + lengths[i]
        lower = jnp.maximum(doc, low * BLK)
        for hh in range(4):
            cols = slice((blk * 4 + hh) * BLK, (blk * 4 + hh + 1) * BLK)
            low_row[:, cols] = lower
            pos_row[:, cols] = pos

    def copy(src, dst, piece, to, k):
        return pltpu.make_async_remote_copy(
            src_ref=kv.at[src, piece],
            dst_ref=kv.at[dst, piece],
            send_sem=send_sem.at[k],
            recv_sem=recv_sem.at[dst, piece],
            device_id=(to, head),
            device_id_type=MESH,
        )

    first_row, last_row = here < 4, here >= shards - 4
    sends = [[0] * 3 for _ in range(4)]
    waited = [set(), set(), set(), set()]

    ALWAYS, CROSS, LATER = range(3)

    def guarded(kind, action):
        if kind == ALWAYS:
            action()
        else:
            pl.when(jnp.logical_not(last_row if kind == CROSS else first_row))(action)

    def send(col, src, dst, piece, to, kind=ALWAYS):
        k = 8 * kind + sends[col][kind]
        sends[col][kind] += 1
        guarded(kind, lambda: copy(src, dst, piece, to, k).start())

    def from_row_before(col, slot):
        return (
            slot in (BACK4, PASS_ROW)
            or (slot == BACK1 and col == 0)
            or (slot == BACK3 and col < 3)
            or (slot == BACK2 and col < 2)
        )

    def arrive(col, slot, piece):
        if (slot, piece) not in waited[col]:
            waited[col].add((slot, piece))
            guarded(
                LATER if from_row_before(col, slot) else ALWAYS,
                lambda: copy(OWN, slot, piece, up, 0).wait_recv(),
            )

    def by_column(step):
        for col in range(4):
            pl.when(z == col)(functools.partial(step, col))

    A, B = (0, 1), (2, 3)

    def send_first(col):
        for a in A:
            send(col, OWN, BACK1 if col < 3 else PASS_UP, a, up)
            send(col, OWN, PASS_DOWN if col > 0 else BACK3, a, down)

    def send_second(col):
        for b in B:
            send(col, OWN, BACK4, b, row_next, CROSS)
            if col < 3:
                send(col, OWN, BACK1, b, up)
            if col == 0:
                send(col, OWN, BACK3, b, down)

    def relay_first(i, col):
        a, b = A[i], B[i]
        if col == 0:
            arrive(col, PASS_DOWN, a)
            send(col, PASS_DOWN, BACK3, a, row_next, CROSS)
            send(col, PASS_DOWN, BACK2, a, down)
            arrive(col, PASS_UP, a)
            send(col, PASS_UP, BACK1, a, row_next, CROSS)
        if col in (1, 2):
            arrive(col, PASS_DOWN, a)
            send(col, PASS_DOWN, BACK3, a, row_next, CROSS)
        if col == 1:
            arrive(col, BACK1, a)
            send(col, BACK1, BACK2, a, up)
        if col == 3:
            arrive(col, BACK1, a)
            send(col, BACK1, PASS_ROW, a, row_next, CROSS)
        if col > 0:
            arrive(col, BACK4, b)
            send(col, BACK4, BACK3, b, down, LATER)
        if col == 3:
            send(col, BACK4, BACK1, b, up, LATER)

    def relay_second(i, col):
        b = B[i]
        if col == 2:
            arrive(col, BACK1, b)
            send(col, BACK1, BACK2, b, up)
        if col == 3:
            arrive(col, BACK3, b)
            send(col, BACK3, BACK2, b, down)

    def relay_third(i, col):
        a, b = A[i], B[i]
        if col == 0:
            arrive(col, BACK1, b)
            send(col, BACK1, BACK2, b, up, LATER)
        if col == 1:
            arrive(col, BACK3, b)
            send(col, BACK3, BACK2, b, down, LATER)
        if col == 2:
            arrive(col, BACK3, a)
            send(col, BACK3, BACK2, a, down, LATER)
        if col == 3:
            arrive(col, PASS_ROW, a)
            send(col, PASS_ROW, BACK2, a, up, LATER)

    def all_of(slots_pieces):
        def step(col):
            for slot, piece in slots_pieces:
                arrive(col, slot, piece)

        by_column(step)

    def mm(x, w):
        return jnp.dot(x, w, preferred_element_type=jnp.float32)

    load_h.wait()
    load_k0.wait()
    kv_sum[:, 0:256] = mm(h_own[...], wk[0])
    load_v0.wait()
    kv_sum[:, 256:512] = mm(h_own[...], wv[0])
    load_q0.wait()

    def q_own(n, _):
        cols = pl.ds(pl.multiple_of(n * 256, 256), 256)
        q_sum[:, cols] = mm(h_own[...], wq[0, :, cols])
        return 0

    lax.fori_loop(0, 2, q_own, 0)

    for blk in range(2):
        swaps[blk].wait_recv()
        if blk == 0:
            load_k1.wait()
            load_v1.wait()
        rows = slice(blk * BLK, (blk + 1) * BLK)
        keys = kv_sum[rows, 0:256] + mm(h_oth[rows], wk[1])
        values = kv_sum[rows, 256:512] + mm(h_oth[rows], wv[1])
        for g in range(2):
            cols = slice(g * HEAD, (g + 1) * HEAD)
            kv[OWN, 2 * blk + g, 0:128] = keys[:, cols].astype(jnp.bfloat16)
            kv[OWN, 2 * blk + g, 128:256] = values[:, cols].T.astype(jnp.bfloat16)
        by_column(send_first if blk == 0 else send_second)

    lax.fori_loop(2, 4, q_own, 0)
    load_q1.wait()

    def q_oth(n, _):
        cols = pl.ds(pl.multiple_of(n * 256, 256), 256)
        q = (q_sum[:, cols] + mm(h_oth[...], wq[1, :, cols])).astype(jnp.bfloat16)
        g, pair = n // 2, lax.rem(n, 2)
        for blk in range(2):
            for j in range(2):
                first = pl.multiple_of((blk * 4 + pair * 2 + j) * BLK, BLK)
                qs[g, :, pl.ds(first, BLK)] = q[blk * BLK : (blk + 1) * BLK, j * HEAD : (j + 1) * HEAD].T
        return 0

    lax.fori_loop(0, 4, q_oth, 0)

    factor = math.log2(math.e) / math.sqrt(HEAD)

    def scores_of(slot, g, chunk, blocks, causal, first, last):
        q = qs[g, :, chunk * 256 : (chunk + 1) * 256]
        for i, (src, blk, _) in enumerate(blocks):
            s_buf[slot, i * BLK : (i + 1) * BLK] = mm(kv[src, 2 * blk + g, 0:128], q)

    def weights_of(slot, g, chunk, blocks, causal, first, last):
        lanes = slice(chunk * 256, (chunk + 1) * 256)
        low = low_row[0:1, lanes]
        parts = []
        for i, (_, blk, back) in enumerate(blocks):
            k_pos = ((here - back) * 2 + blk) * BLK + lax.broadcasted_iota(
                jnp.int32, (BLK, 256), 0
            )
            allowed = k_pos >= low
            if causal:
                allowed = allowed & (k_pos <= pos_row[0:1, lanes])
            parts.append(jnp.where(allowed, s_buf[slot, i * BLK : (i + 1) * BLK] * factor, NEG))
        top = functools.reduce(jnp.maximum, [p.reshape(BLK // 8, 8, 256).max(axis=0) for p in parts])
        top = jnp.max(top, axis=0, keepdims=True)
        if not first:
            old = m_s[g, 0:1, lanes]
            top = jnp.maximum(old, top)
            shrink = jnp.exp2(old - top)
            shrink_s[slot, 0:1] = shrink
        if not last:
            m_s[g, 0:1, lanes] = top
        total = None
        for i, s in enumerate(parts):
            p = jnp.exp2(s - top)
            p_buf[slot, i * BLK : (i + 1) * BLK] = p.astype(jnp.bfloat16)
            p = p.reshape(BLK // 8, 8, 256).sum(axis=0)
            total = p if total is None else total + p
        l_s[g, :, lanes] = total if first else total + l_s[g, :, lanes] * shrink

    def mix_of(slot, g, chunk, blocks, causal, first, last):
        lanes = slice(chunk * 256, (chunk + 1) * 256)
        values = jnp.concatenate([kv[src, 2 * blk + g, 128:256] for src, blk, _ in blocks], axis=1)
        mixed = mm(values, p_buf[slot, 0 : len(blocks) * BLK])
        if not first:
            mixed = mixed + acc_s[g, :, lanes] * shrink_s[slot, 0:1]
        if not last:
            acc_s[g, :, lanes] = mixed
            return
        mixed = mixed / jnp.sum(l_s[g, :, lanes], axis=0, keepdims=True)
        rows = slice(chunk // 2 * BLK, (chunk // 2 + 1) * BLK)
        for j in range(2):
            at = g * 4 + chunk % 2 * 2 + j
            out[rows, at * HEAD : (at + 1) * HEAD] = (
                mixed[:, j * HEAD : (j + 1) * HEAD].T.astype(jnp.bfloat16)
            )

    def run(tasks):
        count = len(tasks)
        for i in range(count + 2):
            for stage, j in ((scores_of, i), (mix_of, i - 2), (weights_of, i - 1)):
                if 0 <= j < count:
                    stage(j % 3, *tasks[j])

    def task(g, chunk, blocks, causal=False, first=False, last=False):
        return g, chunk, blocks, causal, first, last

    own = [(OWN, 0, 0), (OWN, 1, 0)]
    for i in range(2):
        by_column(functools.partial(relay_first, i))
    run(
        [
            task(g, chunk, own[: 1 + chunk // 2], causal=True, first=True)
            for g in range(2)
            for chunk in range(4)
        ]
    )

    for i in range(2):
        by_column(functools.partial(relay_second, i))
        by_column(functools.partial(relay_third, i))

    all_of([(BACK1, piece) for piece in range(4)])
    back1 = [(BACK1, 0, 1), (BACK1, 1, 1)]
    run([task(g, chunk, back1) for g in range(2) for chunk in range(4)])
    all_of([(BACK3, piece) for piece in range(4)] + [(BACK4, b) for b in B])
    back3 = [(BACK4, 1, 4), (BACK3, 0, 3), (BACK3, 1, 3)]
    run([task(g, chunk, back3[chunk // 2 * 2 :]) for g in range(2) for chunk in range(4)])
    back2 = [(BACK2, 0, 2), (BACK2, 1, 2)]
    for g in range(2):
        all_of([(BACK2, g), (BACK2, 2 + g)])
        run([task(g, chunk, back2, last=True) for chunk in range(4)])

    for swap in swaps:
        swap.wait_send()

    def finish(col):
        for kind in range(3):
            for k in range(sends[col][kind]):
                guarded(kind, lambda k=8 * kind + k: copy(OWN, BACK1, 0, up, k).wait_send())

    by_column(finish)


def local(hidden, block_owner, doc_lengths, w_query, w_key, value_weight):
    rows, half = hidden.shape
    q_cols, k_cols = w_query.shape[1], w_key.shape[1]
    groups = k_cols // HEAD
    shards = lax.axis_size("ctx")
    bf16, f32 = jnp.bfloat16, jnp.float32
    lanes = rows * q_cols // k_cols
    dma = pltpu.SemaphoreType.DMA
    any_spec = pl.BlockSpec(memory_space=pl.ANY)
    macs = rows * 2 * half * (q_cols + 2 * k_cols)
    return pl.pallas_call(
        functools.partial(kernel, shards),
        out_shape=pltpu.VMEM((rows, q_cols), bf16),
        in_specs=[any_spec] * 6,
        out_specs=pl.BlockSpec(memory_space=pltpu.VMEM),
        scratch_shapes=[
            pltpu.SMEM(block_owner.shape, jnp.int32),
            pltpu.SMEM(doc_lengths.shape, jnp.int32),
            pltpu.VMEM((rows, half), bf16),
            pltpu.VMEM((rows, half), bf16),
            pltpu.VMEM((2, half, q_cols), bf16),
            pltpu.VMEM((2, half, k_cols), bf16),
            pltpu.VMEM((2, half, k_cols), bf16),
            pltpu.VMEM((rows, 2 * k_cols), f32),
            pltpu.VMEM((rows, q_cols), f32),
            pltpu.VMEM((groups, HEAD, lanes), bf16),
            pltpu.VMEM((8, 4, 2 * BLK, HEAD), bf16),
            pltpu.VMEM((8, lanes), jnp.int32),
            pltpu.VMEM((8, lanes), jnp.int32),
            pltpu.VMEM((groups, 8, lanes), f32),
            pltpu.VMEM((groups, 8, lanes), f32),
            pltpu.VMEM((groups, HEAD, lanes), f32),
            pltpu.VMEM((3, 3 * BLK, 256), f32),
            pltpu.VMEM((3, 3 * BLK, 256), bf16),
            pltpu.VMEM((3, 8, 256), f32),
            dma((9,)),
            dma((2,)),
            dma((2,)),
            dma((24,)),
            dma((8, 4)),
        ],
        compiler_params=pltpu.CompilerParams(
            collective_id=0, has_side_effects=True, vmem_limit_bytes=56 << 20
        ),
        cost_estimate=pl.CostEstimate(
            flops=4 * macs, bytes_accessed=16 << 20, transcendentals=2 << 20
        ),
        name="attention",
    )(hidden, block_owner, doc_lengths, w_query, w_key, value_weight)


def solution(mesh):
    in_specs = (P("ctx", "head"), P(), P(), P(None, "head"), P(None, "head"), P(None, "head"))
    out_specs = P("ctx", "head")
    return jax.shard_map(local, mesh=mesh, in_specs=in_specs, out_specs=out_specs, check_vma=False)
```

```python
import functools
import math

import jax
import jax.numpy as jnp
from jax import lax
from jax.experimental import pallas as pl
from jax.experimental.pallas import tpu as pltpu
from jax.sharding import PartitionSpec as P

HEAD = 128
BLK = 128
REACH = 2
NEG = -1e30
MESH = pl.DeviceIdType.MESH
OWN, BACK1, BACK3, BACK2, BACK4, PASS_UP, PASS_DOWN, PASS_ROW = range(8)


def kernel(
    shards,
    hid,
    owner_hbm,
    lengths_hbm,
    w_q,
    w_k,
    w_v,
    out,
    owner,
    lengths,
    h_own,
    h_oth,
    wq,
    wk,
    wv,
    kv_sum,
    q_sum,
    qs,
    kv,
    low_row,
    pos_row,
    m_s,
    l_s,
    acc_s,
    s_buf,
    p_buf,
    shrink_s,
    load_sem,
    hid_send,
    hid_recv,
    send_sem,
    recv_sem,
):
    here = lax.axis_index("ctx")
    head = lax.axis_index("head")
    z = lax.rem(here, 4)
    ring = here - z
    up = ring + lax.rem(z + 1, 4)
    down = ring + lax.rem(z + 3, 4)
    row_next = lax.rem(here + 4, shards)
    row_prev = lax.rem(here + shards - 4, shards)
    half = h_own.shape[1]
    mine = pl.multiple_of(head * half, half)
    other = pl.multiple_of((1 - head) * half, half)

    loads = [pltpu.make_async_copy(hid, h_own, load_sem.at[0])]
    for part, first in ((0, mine), (1, other)):
        for src, dst in ((w_k, wk), (w_v, wv)):
            loads.append(
                pltpu.make_async_copy(
                    src.at[pl.ds(first, half)], dst.at[part], load_sem.at[len(loads)]
                )
            )
    for part, first in ((0, mine), (1, other)):
        loads.append(
            pltpu.make_async_copy(
                w_q.at[pl.ds(first, half)], wq.at[part], load_sem.at[len(loads)]
            )
        )
    tables = [
        pltpu.make_async_copy(owner_hbm, owner, load_sem.at[7]),
        pltpu.make_async_copy(lengths_hbm, lengths, load_sem.at[8]),
    ]
    for load in tables + loads:
        load.start()
    load_h, load_k0, load_v0, load_k1, load_v1, load_q0, load_q1 = loads

    @pl.when(here < 4)
    def _():
        for slot in (BACK1, BACK3, BACK2, BACK4):
            kv[slot] = jnp.zeros(kv.shape[1:], kv.dtype)

    barrier = pltpu.get_barrier_semaphore()
    for peer in ((here, 1 - head), (up, head), (down, head), (row_prev, head)):
        pl.semaphore_signal(barrier, inc=1, device_id=peer, device_id_type=MESH)
    pl.semaphore_wait(barrier, 4)

    swaps = []
    for blk in range(2):
        rows = pl.ds(blk * BLK, BLK)
        swaps.append(
            pltpu.make_async_remote_copy(
                src_ref=hid.at[rows],
                dst_ref=h_oth.at[rows],
                send_sem=hid_send.at[blk],
                recv_sem=hid_recv.at[blk],
                device_id=(here, 1 - head),
                device_id_type=MESH,
            )
        )
        swaps[-1].start()

    for table in tables:
        table.wait()
    first_block = 2 * here - 8
    lane = lax.broadcasted_iota(jnp.int32, (8, BLK), 1)
    for blk in range(2):
        shard = owner[2 * here + blk]
        low = jnp.maximum(first_block, 0)
        for j in range(10):
            block = first_block + j
            below = owner[jnp.maximum(block, 0)] < shard - REACH
            low = low + jnp.where(below & (block >= 0), 1, 0)
        pos = (2 * here + blk) * BLK + lane
        start = jnp.int32(0)
        doc = jnp.zeros((8, BLK), jnp.int32)
        for i in range(lengths.shape[0]):
            doc = jnp.where(pos >= start, start, doc)
            start = start + lengths[i]
        lower = jnp.maximum(doc, low * BLK)
        for hh in range(4):
            cols = slice((blk * 4 + hh) * BLK, (blk * 4 + hh + 1) * BLK)
            low_row[:, cols] = lower
            pos_row[:, cols] = pos

    def copy(src, dst, piece, to, k):
        return pltpu.make_async_remote_copy(
            src_ref=kv.at[src, piece],
            dst_ref=kv.at[dst, piece],
            send_sem=send_sem.at[k],
            recv_sem=recv_sem.at[dst, piece],
            device_id=(to, head),
            device_id_type=MESH,
        )

    first_row, last_row = here < 4, here >= shards - 4
    sends = [[0] * 3 for _ in range(4)]
    waited = [set(), set(), set(), set()]

    ALWAYS, CROSS, LATER = range(3)

    def guarded(kind, action):
        if kind == ALWAYS:
            action()
        else:
            pl.when(jnp.logical_not(last_row if kind == CROSS else first_row))(action)

    def send(col, src, dst, piece, to, kind=ALWAYS):
        k = 8 * kind + sends[col][kind]
        sends[col][kind] += 1
        guarded(kind, lambda: copy(src, dst, piece, to, k).start())

    def from_row_before(col, slot):
        return (
            slot in (BACK4, PASS_ROW)
            or (slot == BACK1 and col == 0)
            or (slot == BACK3 and col < 3)
            or (slot == BACK2 and col < 2)
        )

    def arrive(col, slot, piece):
        if (slot, piece) not in waited[col]:
            waited[col].add((slot, piece))
            guarded(
                LATER if from_row_before(col, slot) else ALWAYS,
                lambda: copy(OWN, slot, piece, up, 0).wait_recv(),
            )

    def by_column(step):
        for col in range(4):
            pl.when(z == col)(functools.partial(step, col))

    A, B = (0, 1), (2, 3)

    def send_first(col):
        for a in A:
            send(col, OWN, BACK1 if col < 3 else PASS_UP, a, up)
            send(col, OWN, PASS_DOWN if col > 0 else BACK3, a, down)

    def send_second(col):
        for b in B:
            send(col, OWN, BACK4, b, row_next, CROSS)
            if col < 3:
                send(col, OWN, BACK1, b, up)
            if col == 0:
                send(col, OWN, BACK3, b, down)

    def relay_first(i, col):
        a, b = A[i], B[i]
        if col == 0:
            arrive(col, PASS_DOWN, a)
            send(col, PASS_DOWN, BACK3, a, row_next, CROSS)
            send(col, PASS_DOWN, BACK2, a, down)
            arrive(col, PASS_UP, a)
            send(col, PASS_UP, BACK1, a, row_next, CROSS)
        if col in (1, 2):
            arrive(col, PASS_DOWN, a)
            send(col, PASS_DOWN, BACK3, a, row_next, CROSS)
        if col == 1:
            arrive(col, BACK1, a)
            send(col, BACK1, BACK2, a, up)
        if col == 3:
            arrive(col, BACK1, a)
            send(col, BACK1, PASS_ROW, a, row_next, CROSS)
        if col > 0:
            arrive(col, BACK4, b)
            send(col, BACK4, BACK3, b, down, LATER)
        if col == 3:
            send(col, BACK4, BACK1, b, up, LATER)

    def relay_second(i, col):
        b = B[i]
        if col == 2:
            arrive(col, BACK1, b)
            send(col, BACK1, BACK2, b, up)
        if col == 3:
            arrive(col, BACK3, b)
            send(col, BACK3, BACK2, b, down)

    def relay_third(i, col):
        a, b = A[i], B[i]
        if col == 0:
            arrive(col, BACK1, b)
            send(col, BACK1, BACK2, b, up, LATER)
        if col == 1:
            arrive(col, BACK3, b)
            send(col, BACK3, BACK2, b, down, LATER)
        if col == 2:
            arrive(col, BACK3, a)
            send(col, BACK3, BACK2, a, down, LATER)
        if col == 3:
            arrive(col, PASS_ROW, a)
            send(col, PASS_ROW, BACK2, a, up, LATER)

    def all_of(slots_pieces):
        def step(col):
            for slot, piece in slots_pieces:
                arrive(col, slot, piece)

        by_column(step)

    def mm(x, w):
        return jnp.dot(x, w, preferred_element_type=jnp.float32)

    load_h.wait()
    load_k0.wait()
    kv_sum[:, 0:256] = mm(h_own[...], wk[0])
    load_v0.wait()
    kv_sum[:, 256:512] = mm(h_own[...], wv[0])
    load_q0.wait()

    def q_own(n, _):
        cols = pl.ds(pl.multiple_of(n * 256, 256), 256)
        q_sum[:, cols] = mm(h_own[...], wq[0, :, cols])
        return 0

    lax.fori_loop(0, 2, q_own, 0)

    for blk in range(2):
        swaps[blk].wait_recv()
        if blk == 0:
            load_k1.wait()
            load_v1.wait()
        rows = slice(blk * BLK, (blk + 1) * BLK)
        keys = kv_sum[rows, 0:256] + mm(h_oth[rows], wk[1])
        values = kv_sum[rows, 256:512] + mm(h_oth[rows], wv[1])
        for g in range(2):
            cols = slice(g * HEAD, (g + 1) * HEAD)
            kv[OWN, 2 * blk + g, 0:128] = keys[:, cols].astype(jnp.bfloat16)
            kv[OWN, 2 * blk + g, 128:256] = values[:, cols].T.astype(jnp.bfloat16)
        by_column(send_first if blk == 0 else send_second)

    lax.fori_loop(2, 4, q_own, 0)
    load_q1.wait()

    def q_oth(n, _):
        cols = pl.ds(pl.multiple_of(n * 256, 256), 256)
        q = (q_sum[:, cols] + mm(h_oth[...], wq[1, :, cols])).astype(jnp.bfloat16)
        g, pair = n // 2, lax.rem(n, 2)
        for blk in range(2):
            for j in range(2):
                first = pl.multiple_of((blk * 4 + pair * 2 + j) * BLK, BLK)
                qs[g, :, pl.ds(first, BLK)] = q[blk * BLK : (blk + 1) * BLK, j * HEAD : (j + 1) * HEAD].T
        return 0

    lax.fori_loop(0, 4, q_oth, 0)

    factor = math.log2(math.e) / math.sqrt(HEAD)

    def scores_of(slot, g, chunk, blocks, causal, first, last):
        q = qs[g, :, chunk * 256 : (chunk + 1) * 256]
        for i, (src, blk, _) in enumerate(blocks):
            s_buf[slot, i * BLK : (i + 1) * BLK] = mm(kv[src, 2 * blk + g, 0:128], q)

    def weights_of(slot, g, chunk, blocks, causal, first, last):
        lanes = slice(chunk * 256, (chunk + 1) * 256)
        low = low_row[0:1, lanes]
        parts = []
        for i, (_, blk, back) in enumerate(blocks):
            k_pos = ((here - back) * 2 + blk) * BLK + lax.broadcasted_iota(
                jnp.int32, (BLK, 256), 0
            )
            allowed = k_pos >= low
            if causal:
                allowed = allowed & (k_pos <= pos_row[0:1, lanes])
            parts.append(jnp.where(allowed, s_buf[slot, i * BLK : (i + 1) * BLK] * factor, NEG))
        top = functools.reduce(jnp.maximum, [p.reshape(BLK // 8, 8, 256).max(axis=0) for p in parts])
        top = jnp.max(top, axis=0, keepdims=True)
        if not first:
            old = m_s[g, 0:1, lanes]
            top = jnp.maximum(old, top)
            shrink = jnp.exp2(old - top)
            shrink_s[slot, 0:1] = shrink
        if not last:
            m_s[g, 0:1, lanes] = top
        total = None
        for i, s in enumerate(parts):
            p = jnp.exp2(s - top)
            p_buf[slot, i * BLK : (i + 1) * BLK] = p.astype(jnp.bfloat16)
            p = p.reshape(BLK // 8, 8, 256).sum(axis=0)
            total = p if total is None else total + p
        l_s[g, :, lanes] = total if first else total + l_s[g, :, lanes] * shrink

    def mix_of(slot, g, chunk, blocks, causal, first, last):
        lanes = slice(chunk * 256, (chunk + 1) * 256)
        values = jnp.concatenate([kv[src, 2 * blk + g, 128:256] for src, blk, _ in blocks], axis=1)
        mixed = mm(values, p_buf[slot, 0 : len(blocks) * BLK])
        if not first:
            mixed = mixed + acc_s[g, :, lanes] * shrink_s[slot, 0:1]
        if not last:
            acc_s[g, :, lanes] = mixed
            return
        mixed = mixed / jnp.sum(l_s[g, :, lanes], axis=0, keepdims=True)
        rows = slice(chunk // 2 * BLK, (chunk // 2 + 1) * BLK)
        for j in range(2):
            at = g * 4 + chunk % 2 * 2 + j
            out[rows, at * HEAD : (at + 1) * HEAD] = (
                mixed[:, j * HEAD : (j + 1) * HEAD].T.astype(jnp.bfloat16)
            )

    def run(tasks):
        count = len(tasks)
        for i in range(count + 2):
            for stage, j in ((scores_of, i), (mix_of, i - 2), (weights_of, i - 1)):
                if 0 <= j < count:
                    stage(j % 3, *tasks[j])

    def task(g, chunk, blocks, causal=False, first=False, last=False):
        return g, chunk, blocks, causal, first, last

    own = [(OWN, 0, 0), (OWN, 1, 0)]
    for i in range(2):
        by_column(functools.partial(relay_first, i))
    run(
        [
            task(g, chunk, own[: 1 + chunk // 2], causal=True, first=True)
            for g in range(2)
            for chunk in range(4)
        ]
    )

    for i in range(2):
        by_column(functools.partial(relay_second, i))
        by_column(functools.partial(relay_third, i))

    all_of([(BACK3, piece) for piece in range(4)] + [(BACK4, b) for b in B])
    back3 = [(BACK4, 1, 4), (BACK3, 0, 3), (BACK3, 1, 3)]
    run([task(g, chunk, back3[chunk // 2 * 2 :]) for g in range(2) for chunk in range(4)])
    all_of([(BACK1, piece) for piece in range(4)])
    back1 = [(BACK1, 0, 1), (BACK1, 1, 1)]
    run([task(g, chunk, back1) for g in range(2) for chunk in range(4)])
    back2 = [(BACK2, 0, 2), (BACK2, 1, 2)]
    for g in range(2):
        all_of([(BACK2, g), (BACK2, 2 + g)])
        run([task(g, chunk, back2, last=True) for chunk in range(4)])

    for swap in swaps:
        swap.wait_send()

    def finish(col):
        for kind in range(3):
            for k in range(sends[col][kind]):
                guarded(kind, lambda k=8 * kind + k: copy(OWN, BACK1, 0, up, k).wait_send())

    by_column(finish)


def local(hidden, block_owner, doc_lengths, w_query, w_key, value_weight):
    rows, half = hidden.shape
    q_cols, k_cols = w_query.shape[1], w_key.shape[1]
    groups = k_cols // HEAD
    shards = lax.axis_size("ctx")
    bf16, f32 = jnp.bfloat16, jnp.float32
    lanes = rows * q_cols // k_cols
    dma = pltpu.SemaphoreType.DMA
    any_spec = pl.BlockSpec(memory_space=pl.ANY)
    macs = rows * 2 * half * (q_cols + 2 * k_cols)
    return pl.pallas_call(
        functools.partial(kernel, shards),
        out_shape=pltpu.VMEM((rows, q_cols), bf16),
        in_specs=[any_spec] * 6,
        out_specs=pl.BlockSpec(memory_space=pltpu.VMEM),
        scratch_shapes=[
            pltpu.SMEM(block_owner.shape, jnp.int32),
            pltpu.SMEM(doc_lengths.shape, jnp.int32),
            pltpu.VMEM((rows, half), bf16),
            pltpu.VMEM((rows, half), bf16),
            pltpu.VMEM((2, half, q_cols), bf16),
            pltpu.VMEM((2, half, k_cols), bf16),
            pltpu.VMEM((2, half, k_cols), bf16),
            pltpu.VMEM((rows, 2 * k_cols), f32),
            pltpu.VMEM((rows, q_cols), f32),
            pltpu.VMEM((groups, HEAD, lanes), bf16),
            pltpu.VMEM((8, 4, 2 * BLK, HEAD), bf16),
            pltpu.VMEM((8, lanes), jnp.int32),
            pltpu.VMEM((8, lanes), jnp.int32),
            pltpu.VMEM((groups, 8, lanes), f32),
            pltpu.VMEM((groups, 8, lanes), f32),
            pltpu.VMEM((groups, HEAD, lanes), f32),
            pltpu.VMEM((3, 3 * BLK, 256), f32),
            pltpu.VMEM((3, 3 * BLK, 256), bf16),
            pltpu.VMEM((3, 8, 256), f32),
            dma((9,)),
            dma((2,)),
            dma((2,)),
            dma((24,)),
            dma((8, 4)),
        ],
        compiler_params=pltpu.CompilerParams(
            collective_id=0, has_side_effects=True, vmem_limit_bytes=56 << 20
        ),
        cost_estimate=pl.CostEstimate(
            flops=4 * macs, bytes_accessed=16 << 20, transcendentals=2 << 20
        ),
        name="attention",
    )(hidden, block_owner, doc_lengths, w_query, w_key, value_weight)


def solution(mesh):
    in_specs = (P("ctx", "head"), P(), P(), P(None, "head"), P(None, "head"), P(None, "head"))
    out_specs = P("ctx", "head")
    return jax.shard_map(local, mesh=mesh, in_specs=in_specs, out_specs=out_specs, check_vma=False)
```

```python
import functools
import math

import jax
import jax.numpy as jnp
from jax import lax
from jax.experimental import pallas as pl
from jax.experimental.pallas import tpu as pltpu
from jax.sharding import PartitionSpec as P

HEAD = 128
BLK = 128
REACH = 2
NEG = -1e30
MESH = pl.DeviceIdType.MESH
OWN, BACK1, BACK3, BACK2, BACK4, PASS_UP, PASS_DOWN, PASS_ROW = range(8)


def kernel(
    shards,
    hid,
    owner_hbm,
    lengths_hbm,
    w_q,
    w_k,
    w_v,
    out,
    owner,
    lengths,
    h_own,
    h_oth,
    wq,
    wk,
    wv,
    kv_sum,
    q_sum,
    qs,
    kv,
    low_row,
    pos_row,
    m_s,
    l_s,
    acc_s,
    s_buf,
    p_buf,
    shrink_s,
    load_sem,
    hid_send,
    hid_recv,
    send_sem,
    recv_sem,
):
    here = lax.axis_index("ctx")
    head = lax.axis_index("head")
    z = lax.rem(here, 4)
    ring = here - z
    up = ring + lax.rem(z + 1, 4)
    down = ring + lax.rem(z + 3, 4)
    row_next = lax.rem(here + 4, shards)
    row_prev = lax.rem(here + shards - 4, shards)
    half = h_own.shape[1]
    mine = pl.multiple_of(head * half, half)
    other = pl.multiple_of((1 - head) * half, half)

    @pl.when(here < 4)
    def _():
        for slot in (BACK1, BACK3, BACK2, BACK4):
            kv[slot] = jnp.zeros(kv.shape[1:], kv.dtype)

    barrier = pltpu.get_barrier_semaphore()
    for peer in ((here, 1 - head), (up, head), (down, head), (row_prev, head)):
        pl.semaphore_signal(barrier, inc=1, device_id=peer, device_id_type=MESH)
    loads = [pltpu.make_async_copy(hid, h_own, load_sem.at[0])]
    for part, first in ((0, mine), (1, other)):
        for src, dst in ((w_k, wk), (w_v, wv)):
            loads.append(
                pltpu.make_async_copy(
                    src.at[pl.ds(first, half)], dst.at[part], load_sem.at[len(loads)]
                )
            )
    for part, first in ((0, mine), (1, other)):
        loads.append(
            pltpu.make_async_copy(
                w_q.at[pl.ds(first, half)], wq.at[part], load_sem.at[len(loads)]
            )
        )
    tables = [
        pltpu.make_async_copy(owner_hbm, owner, load_sem.at[7]),
        pltpu.make_async_copy(lengths_hbm, lengths, load_sem.at[8]),
    ]
    for load in tables + loads:
        load.start()
    load_h, load_k0, load_v0, load_k1, load_v1, load_q0, load_q1 = loads

    pl.semaphore_wait(barrier, 4)

    swaps = []
    for blk in range(2):
        rows = pl.ds(blk * BLK, BLK)
        swaps.append(
            pltpu.make_async_remote_copy(
                src_ref=hid.at[rows],
                dst_ref=h_oth.at[rows],
                send_sem=hid_send.at[blk],
                recv_sem=hid_recv.at[blk],
                device_id=(here, 1 - head),
                device_id_type=MESH,
            )
        )
        swaps[-1].start()

    for table in tables:
        table.wait()
    first_block = 2 * here - 8
    lane = lax.broadcasted_iota(jnp.int32, (8, BLK), 1)
    for blk in range(2):
        shard = owner[2 * here + blk]
        low = jnp.maximum(first_block, 0)
        for j in range(10):
            block = first_block + j
            below = owner[jnp.maximum(block, 0)] < shard - REACH
            low = low + jnp.where(below & (block >= 0), 1, 0)
        pos = (2 * here + blk) * BLK + lane
        start = jnp.int32(0)
        doc = jnp.zeros((8, BLK), jnp.int32)
        for i in range(lengths.shape[0]):
            doc = jnp.where(pos >= start, start, doc)
            start = start + lengths[i]
        lower = jnp.maximum(doc, low * BLK)
        for hh in range(4):
            cols = slice((blk * 4 + hh) * BLK, (blk * 4 + hh + 1) * BLK)
            low_row[:, cols] = lower
            pos_row[:, cols] = pos

    def copy(src, dst, piece, to, k):
        return pltpu.make_async_remote_copy(
            src_ref=kv.at[src, piece],
            dst_ref=kv.at[dst, piece],
            send_sem=send_sem.at[k],
            recv_sem=recv_sem.at[dst, piece],
            device_id=(to, head),
            device_id_type=MESH,
        )

    first_row, last_row = here < 4, here >= shards - 4
    sends = [[0] * 3 for _ in range(4)]
    waited = [set(), set(), set(), set()]

    ALWAYS, CROSS, LATER = range(3)

    def guarded(kind, action):
        if kind == ALWAYS:
            action()
        else:
            pl.when(jnp.logical_not(last_row if kind == CROSS else first_row))(action)

    def send(col, src, dst, piece, to, kind=ALWAYS):
        k = 8 * kind + sends[col][kind]
        sends[col][kind] += 1
        guarded(kind, lambda: copy(src, dst, piece, to, k).start())

    def from_row_before(col, slot):
        return (
            slot in (BACK4, PASS_ROW)
            or (slot == BACK1 and col == 0)
            or (slot == BACK3 and col < 3)
            or (slot == BACK2 and col < 2)
        )

    def arrive(col, slot, piece):
        if (slot, piece) not in waited[col]:
            waited[col].add((slot, piece))
            guarded(
                LATER if from_row_before(col, slot) else ALWAYS,
                lambda: copy(OWN, slot, piece, up, 0).wait_recv(),
            )

    def by_column(step):
        for col in range(4):
            pl.when(z == col)(functools.partial(step, col))

    A, B = (0, 1), (2, 3)

    def send_first(col):
        for a in A:
            send(col, OWN, BACK1 if col < 3 else PASS_UP, a, up)
            send(col, OWN, PASS_DOWN if col > 0 else BACK3, a, down)

    def send_second(col):
        for b in B:
            send(col, OWN, BACK4, b, row_next, CROSS)
            if col < 3:
                send(col, OWN, BACK1, b, up)
            if col == 0:
                send(col, OWN, BACK3, b, down)

    def relay_first(i, col):
        a, b = A[i], B[i]
        if col == 0:
            arrive(col, PASS_DOWN, a)
            send(col, PASS_DOWN, BACK3, a, row_next, CROSS)
            send(col, PASS_DOWN, BACK2, a, down)
            arrive(col, PASS_UP, a)
            send(col, PASS_UP, BACK1, a, row_next, CROSS)
        if col in (1, 2):
            arrive(col, PASS_DOWN, a)
            send(col, PASS_DOWN, BACK3, a, row_next, CROSS)
        if col == 1:
            arrive(col, BACK1, a)
            send(col, BACK1, BACK2, a, up)
        if col == 3:
            arrive(col, BACK1, a)
            send(col, BACK1, PASS_ROW, a, row_next, CROSS)
        if col > 0:
            arrive(col, BACK4, b)
            send(col, BACK4, BACK3, b, down, LATER)
        if col == 3:
            send(col, BACK4, BACK1, b, up, LATER)

    def relay_second(i, col):
        b = B[i]
        if col == 2:
            arrive(col, BACK1, b)
            send(col, BACK1, BACK2, b, up)
        if col == 3:
            arrive(col, BACK3, b)
            send(col, BACK3, BACK2, b, down)

    def relay_third(i, col):
        a, b = A[i], B[i]
        if col == 0:
            arrive(col, BACK1, b)
            send(col, BACK1, BACK2, b, up, LATER)
        if col == 1:
            arrive(col, BACK3, b)
            send(col, BACK3, BACK2, b, down, LATER)
        if col == 2:
            arrive(col, BACK3, a)
            send(col, BACK3, BACK2, a, down, LATER)
        if col == 3:
            arrive(col, PASS_ROW, a)
            send(col, PASS_ROW, BACK2, a, up, LATER)

    def all_of(slots_pieces):
        def step(col):
            for slot, piece in slots_pieces:
                arrive(col, slot, piece)

        by_column(step)

    def mm(x, w):
        return jnp.dot(x, w, preferred_element_type=jnp.float32)

    load_h.wait()
    load_k0.wait()
    kv_sum[:, 0:256] = mm(h_own[...], wk[0])
    load_v0.wait()
    kv_sum[:, 256:512] = mm(h_own[...], wv[0])

    for blk in range(2):
        swaps[blk].wait_recv()
        if blk == 0:
            load_k1.wait()
            load_v1.wait()
        rows = slice(blk * BLK, (blk + 1) * BLK)
        keys = kv_sum[rows, 0:256] + mm(h_oth[rows], wk[1])
        values = kv_sum[rows, 256:512] + mm(h_oth[rows], wv[1])
        for g in range(2):
            cols = slice(g * HEAD, (g + 1) * HEAD)
            kv[OWN, 2 * blk + g, 0:128] = keys[:, cols].astype(jnp.bfloat16)
            kv[OWN, 2 * blk + g, 128:256] = values[:, cols].T.astype(jnp.bfloat16)
        by_column(send_first if blk == 0 else send_second)

    load_q0.wait()

    def q_own(n, _):
        cols = pl.ds(pl.multiple_of(n * 256, 256), 256)
        q_sum[:, cols] = mm(h_own[...], wq[0, :, cols])
        return 0

    lax.fori_loop(0, 4, q_own, 0)
    load_q1.wait()

    def q_oth(n, _):
        cols = pl.ds(pl.multiple_of(n * 256, 256), 256)
        q = (q_sum[:, cols] + mm(h_oth[...], wq[1, :, cols])).astype(jnp.bfloat16)
        g, pair = n // 2, lax.rem(n, 2)
        for blk in range(2):
            for j in range(2):
                first = pl.multiple_of((blk * 4 + pair * 2 + j) * BLK, BLK)
                qs[g, :, pl.ds(first, BLK)] = q[blk * BLK : (blk + 1) * BLK, j * HEAD : (j + 1) * HEAD].T
        return 0

    lax.fori_loop(0, 1, q_oth, 0)

    factor = math.log2(math.e) / math.sqrt(HEAD)

    def scores_of(slot, g, chunk, blocks, causal, first, last):
        q = qs[g, :, chunk * 256 : (chunk + 1) * 256]
        for i, (src, blk, _) in enumerate(blocks):
            s_buf[slot, i * BLK : (i + 1) * BLK] = mm(kv[src, 2 * blk + g, 0:128], q)

    def weights_of(slot, g, chunk, blocks, causal, first, last):
        lanes = slice(chunk * 256, (chunk + 1) * 256)
        low = low_row[0:1, lanes]
        parts = []
        for i, (_, blk, back) in enumerate(blocks):
            k_pos = ((here - back) * 2 + blk) * BLK + lax.broadcasted_iota(
                jnp.int32, (BLK, 256), 0
            )
            allowed = k_pos >= low
            if causal:
                allowed = allowed & (k_pos <= pos_row[0:1, lanes])
            parts.append(jnp.where(allowed, s_buf[slot, i * BLK : (i + 1) * BLK] * factor, NEG))
        top = functools.reduce(jnp.maximum, [p.reshape(BLK // 8, 8, 256).max(axis=0) for p in parts])
        top = jnp.max(top, axis=0, keepdims=True)
        if not first:
            old = m_s[g, 0:1, lanes]
            top = jnp.maximum(old, top)
            shrink = jnp.exp2(old - top)
            shrink_s[slot, 0:1] = shrink
        if not last:
            m_s[g, 0:1, lanes] = top
        total = None
        for i, s in enumerate(parts):
            p = jnp.exp2(s - top)
            p_buf[slot, i * BLK : (i + 1) * BLK] = p.astype(jnp.bfloat16)
            p = p.reshape(BLK // 8, 8, 256).sum(axis=0)
            total = p if total is None else total + p
        l_s[g, :, lanes] = total if first else total + l_s[g, :, lanes] * shrink

    def mix_of(slot, g, chunk, blocks, causal, first, last):
        lanes = slice(chunk * 256, (chunk + 1) * 256)
        values = jnp.concatenate([kv[src, 2 * blk + g, 128:256] for src, blk, _ in blocks], axis=1)
        mixed = mm(values, p_buf[slot, 0 : len(blocks) * BLK])
        if not first:
            mixed = mixed + acc_s[g, :, lanes] * shrink_s[slot, 0:1]
        if not last:
            acc_s[g, :, lanes] = mixed
            return
        mixed = mixed / jnp.sum(l_s[g, :, lanes], axis=0, keepdims=True)
        rows = slice(chunk // 2 * BLK, (chunk // 2 + 1) * BLK)
        for j in range(2):
            at = g * 4 + chunk % 2 * 2 + j
            out[rows, at * HEAD : (at + 1) * HEAD] = (
                mixed[:, j * HEAD : (j + 1) * HEAD].T.astype(jnp.bfloat16)
            )

    def run(tasks):
        count = len(tasks)
        for i in range(count + 2):
            for stage, j in ((scores_of, i), (mix_of, i - 2), (weights_of, i - 1)):
                if 0 <= j < count:
                    stage(j % 3, *tasks[j])

    def task(g, chunk, blocks, causal=False, first=False, last=False):
        return g, chunk, blocks, causal, first, last

    own = [(OWN, 0, 0), (OWN, 1, 0)]
    by_column(functools.partial(relay_first, 0))
    lax.fori_loop(1, 4, q_oth, 0)
    by_column(functools.partial(relay_first, 1))
    for i in range(2):
        run([task(i, chunk, own[: 1 + chunk // 2], causal=True, first=True) for chunk in range(4)])
        by_column(functools.partial(relay_second, i))
        by_column(functools.partial(relay_third, i))

    all_of([(BACK3, piece) for piece in range(4)] + [(BACK4, b) for b in B])
    back3 = [(BACK4, 1, 4), (BACK3, 0, 3), (BACK3, 1, 3)]
    run([task(g, chunk, back3[chunk // 2 * 2 :]) for g in range(2) for chunk in range(4)])
    all_of([(BACK1, piece) for piece in range(4)])
    back1 = [(BACK1, 0, 1), (BACK1, 1, 1)]
    run([task(g, chunk, back1) for g in range(2) for chunk in range(4)])
    back2 = [(BACK2, 0, 2), (BACK2, 1, 2)]
    for g in range(2):
        all_of([(BACK2, g), (BACK2, 2 + g)])
        run([task(g, chunk, back2, last=True) for chunk in range(4)])

    for swap in swaps:
        swap.wait_send()

    def finish(col):
        for kind in range(3):
            for k in range(sends[col][kind]):
                guarded(kind, lambda k=8 * kind + k: copy(OWN, BACK1, 0, up, k).wait_send())

    by_column(finish)


def local(hidden, block_owner, doc_lengths, w_query, w_key, value_weight):
    rows, half = hidden.shape
    q_cols, k_cols = w_query.shape[1], w_key.shape[1]
    groups = k_cols // HEAD
    shards = lax.axis_size("ctx")
    bf16, f32 = jnp.bfloat16, jnp.float32
    lanes = rows * q_cols // k_cols
    dma = pltpu.SemaphoreType.DMA
    any_spec = pl.BlockSpec(memory_space=pl.ANY)
    macs = rows * 2 * half * (q_cols + 2 * k_cols)
    return pl.pallas_call(
        functools.partial(kernel, shards),
        out_shape=pltpu.VMEM((rows, q_cols), bf16),
        in_specs=[any_spec] * 6,
        out_specs=pl.BlockSpec(memory_space=pltpu.VMEM),
        scratch_shapes=[
            pltpu.SMEM(block_owner.shape, jnp.int32),
            pltpu.SMEM(doc_lengths.shape, jnp.int32),
            pltpu.VMEM((rows, half), bf16),
            pltpu.VMEM((rows, half), bf16),
            pltpu.VMEM((2, half, q_cols), bf16),
            pltpu.VMEM((2, half, k_cols), bf16),
            pltpu.VMEM((2, half, k_cols), bf16),
            pltpu.VMEM((rows, 2 * k_cols), f32),
            pltpu.VMEM((rows, q_cols), f32),
            pltpu.VMEM((groups, HEAD, lanes), bf16),
            pltpu.VMEM((8, 4, 2 * BLK, HEAD), bf16),
            pltpu.VMEM((8, lanes), jnp.int32),
            pltpu.VMEM((8, lanes), jnp.int32),
            pltpu.VMEM((groups, 8, lanes), f32),
            pltpu.VMEM((groups, 8, lanes), f32),
            pltpu.VMEM((groups, HEAD, lanes), f32),
            pltpu.VMEM((3, 3 * BLK, 256), f32),
            pltpu.VMEM((3, 3 * BLK, 256), bf16),
            pltpu.VMEM((3, 8, 256), f32),
            dma((9,)),
            dma((2,)),
            dma((2,)),
            dma((24,)),
            dma((8, 4)),
        ],
        compiler_params=pltpu.CompilerParams(
            collective_id=0, has_side_effects=True, vmem_limit_bytes=56 << 20
        ),
        cost_estimate=pl.CostEstimate(
            flops=4 * macs, bytes_accessed=16 << 20, transcendentals=2 << 20
        ),
        name="attention",
    )(hidden, block_owner, doc_lengths, w_query, w_key, value_weight)


def solution(mesh):
    in_specs = (P("ctx", "head"), P(), P(), P(None, "head"), P(None, "head"), P(None, "head"))
    out_specs = P("ctx", "head")
    return jax.shard_map(local, mesh=mesh, in_specs=in_specs, out_specs=out_specs, check_vma=False)
```

```python
import functools
import math

import jax
import jax.numpy as jnp
from jax import lax
from jax.experimental import pallas as pl
from jax.experimental.pallas import tpu as pltpu
from jax.sharding import PartitionSpec as P

HEAD = 128
BLK = 128
REACH = 2
NEG = -1e30
MESH = pl.DeviceIdType.MESH
OWN, BACK1, BACK3, BACK2, BACK4, PASS_UP, PASS_DOWN, PASS_ROW = range(8)


def kernel(
    shards,
    hid,
    owner_hbm,
    lengths_hbm,
    w_q,
    w_k,
    w_v,
    out,
    owner,
    lengths,
    h_own,
    h_oth,
    wq,
    wk,
    wv,
    kv_sum,
    q_sum,
    qs,
    kv,
    low_row,
    pos_row,
    m_s,
    l_s,
    acc_s,
    s_buf,
    p_buf,
    shrink_s,
    load_sem,
    hid_send,
    hid_recv,
    send_sem,
    recv_sem,
):
    here = lax.axis_index("ctx")
    head = lax.axis_index("head")
    z = lax.rem(here, 4)
    ring = here - z
    up = ring + lax.rem(z + 1, 4)
    down = ring + lax.rem(z + 3, 4)
    row_next = lax.rem(here + 4, shards)
    row_prev = lax.rem(here + shards - 4, shards)
    half = h_own.shape[1]
    mine = pl.multiple_of(head * half, half)
    other = pl.multiple_of((1 - head) * half, half)

    @pl.when(here < 4)
    def _():
        for slot in (BACK1, BACK3, BACK2, BACK4):
            kv[slot] = jnp.zeros(kv.shape[1:], kv.dtype)

    barrier = pltpu.get_barrier_semaphore()
    for peer in ((here, 1 - head), (up, head), (down, head), (row_prev, head)):
        pl.semaphore_signal(barrier, inc=1, device_id=peer, device_id_type=MESH)
    loads = [pltpu.make_async_copy(hid, h_own, load_sem.at[0])]
    for part, first in ((0, mine), (1, other)):
        for src, dst in ((w_k, wk), (w_v, wv)):
            loads.append(
                pltpu.make_async_copy(
                    src.at[pl.ds(first, half)], dst.at[part], load_sem.at[len(loads)]
                )
            )
    for part, first in ((0, mine), (1, other)):
        loads.append(
            pltpu.make_async_copy(
                w_q.at[pl.ds(first, half)], wq.at[part], load_sem.at[len(loads)]
            )
        )
    tables = [
        pltpu.make_async_copy(owner_hbm, owner, load_sem.at[7]),
        pltpu.make_async_copy(lengths_hbm, lengths, load_sem.at[8]),
    ]
    for load in tables + loads[:5]:
        load.start()
    load_h, load_k0, load_v0, load_k1, load_v1, load_q0, load_q1 = loads

    pl.semaphore_wait(barrier, 4)

    swaps = []
    for blk in range(2):
        rows = pl.ds(blk * BLK, BLK)
        swaps.append(
            pltpu.make_async_remote_copy(
                src_ref=hid.at[rows],
                dst_ref=h_oth.at[rows],
                send_sem=hid_send.at[blk],
                recv_sem=hid_recv.at[blk],
                device_id=(here, 1 - head),
                device_id_type=MESH,
            )
        )
        swaps[-1].start()
    load_q0.start()
    load_q1.start()

    for table in tables:
        table.wait()
    first_block = 2 * here - 8
    lane = lax.broadcasted_iota(jnp.int32, (8, BLK), 1)
    for blk in range(2):
        shard = owner[2 * here + blk]
        low = jnp.maximum(first_block, 0)
        for j in range(10):
            block = first_block + j
            below = owner[jnp.maximum(block, 0)] < shard - REACH
            low = low + jnp.where(below & (block >= 0), 1, 0)
        pos = (2 * here + blk) * BLK + lane
        start = jnp.int32(0)
        doc = jnp.zeros((8, BLK), jnp.int32)
        for i in range(lengths.shape[0]):
            doc = jnp.where(pos >= start, start, doc)
            start = start + lengths[i]
        lower = jnp.maximum(doc, low * BLK)
        for hh in range(4):
            cols = slice((blk * 4 + hh) * BLK, (blk * 4 + hh + 1) * BLK)
            low_row[:, cols] = lower
            pos_row[:, cols] = pos

    def copy(src, dst, piece, to, k):
        return pltpu.make_async_remote_copy(
            src_ref=kv.at[src, piece],
            dst_ref=kv.at[dst, piece],
            send_sem=send_sem.at[k],
            recv_sem=recv_sem.at[dst, piece],
            device_id=(to, head),
            device_id_type=MESH,
        )

    first_row, last_row = here < 4, here >= shards - 4
    sends = [[0] * 3 for _ in range(4)]
    waited = [set(), set(), set(), set()]

    ALWAYS, CROSS, LATER = range(3)

    def guarded(kind, action):
        if kind == ALWAYS:
            action()
        else:
            pl.when(jnp.logical_not(last_row if kind == CROSS else first_row))(action)

    def send(col, src, dst, piece, to, kind=ALWAYS):
        k = 8 * kind + sends[col][kind]
        sends[col][kind] += 1
        guarded(kind, lambda: copy(src, dst, piece, to, k).start())

    def from_row_before(col, slot):
        return (
            slot in (BACK4, PASS_ROW)
            or (slot == BACK1 and col == 0)
            or (slot == BACK3 and col < 3)
            or (slot == BACK2 and col < 2)
        )

    def arrive(col, slot, piece):
        if (slot, piece) not in waited[col]:
            waited[col].add((slot, piece))
            guarded(
                LATER if from_row_before(col, slot) else ALWAYS,
                lambda: copy(OWN, slot, piece, up, 0).wait_recv(),
            )

    def by_column(step):
        for col in range(4):
            pl.when(z == col)(functools.partial(step, col))

    A, B = (0, 1), (2, 3)

    def send_first(col):
        for a in A:
            send(col, OWN, BACK1 if col < 3 else PASS_UP, a, up)
            send(col, OWN, PASS_DOWN if col > 0 else BACK3, a, down)

    def send_second(col):
        for b in B:
            send(col, OWN, BACK4, b, row_next, CROSS)
            if col < 3:
                send(col, OWN, BACK1, b, up)
            if col == 0:
                send(col, OWN, BACK3, b, down)

    def relay_first(i, col):
        a, b = A[i], B[i]
        if col == 0:
            arrive(col, PASS_DOWN, a)
            send(col, PASS_DOWN, BACK3, a, row_next, CROSS)
            send(col, PASS_DOWN, BACK2, a, down)
            arrive(col, PASS_UP, a)
            send(col, PASS_UP, BACK1, a, row_next, CROSS)
        if col in (1, 2):
            arrive(col, PASS_DOWN, a)
            send(col, PASS_DOWN, BACK3, a, row_next, CROSS)
        if col == 1:
            arrive(col, BACK1, a)
            send(col, BACK1, BACK2, a, up)
        if col == 3:
            arrive(col, BACK1, a)
            send(col, BACK1, PASS_ROW, a, row_next, CROSS)
        if col > 0:
            arrive(col, BACK4, b)
            send(col, BACK4, BACK3, b, down, LATER)
        if col == 3:
            send(col, BACK4, BACK1, b, up, LATER)

    def relay_second(i, col):
        b = B[i]
        if col == 2:
            arrive(col, BACK1, b)
            send(col, BACK1, BACK2, b, up)
        if col == 3:
            arrive(col, BACK3, b)
            send(col, BACK3, BACK2, b, down)

    def relay_third(i, col):
        a, b = A[i], B[i]
        if col == 0:
            arrive(col, BACK1, b)
            send(col, BACK1, BACK2, b, up, LATER)
        if col == 1:
            arrive(col, BACK3, b)
            send(col, BACK3, BACK2, b, down, LATER)
        if col == 2:
            arrive(col, BACK3, a)
            send(col, BACK3, BACK2, a, down, LATER)
        if col == 3:
            arrive(col, PASS_ROW, a)
            send(col, PASS_ROW, BACK2, a, up, LATER)

    def all_of(slots_pieces):
        def step(col):
            for slot, piece in slots_pieces:
                arrive(col, slot, piece)

        by_column(step)

    def mm(x, w):
        return jnp.dot(x, w, preferred_element_type=jnp.float32)

    load_h.wait()
    load_k0.wait()
    kv_sum[:, 0:256] = mm(h_own[...], wk[0])
    load_v0.wait()
    kv_sum[:, 256:512] = mm(h_own[...], wv[0])

    for blk in range(2):
        swaps[blk].wait_recv()
        if blk == 0:
            load_k1.wait()
            load_v1.wait()
        rows = slice(blk * BLK, (blk + 1) * BLK)
        keys = kv_sum[rows, 0:256] + mm(h_oth[rows], wk[1])
        values = kv_sum[rows, 256:512] + mm(h_oth[rows], wv[1])
        for g in range(2):
            cols = slice(g * HEAD, (g + 1) * HEAD)
            kv[OWN, 2 * blk + g, 0:128] = keys[:, cols].astype(jnp.bfloat16)
            kv[OWN, 2 * blk + g, 128:256] = values[:, cols].T.astype(jnp.bfloat16)
        by_column(send_first if blk == 0 else send_second)

    load_q0.wait()

    def q_own(n, _):
        cols = pl.ds(pl.multiple_of(n * 256, 256), 256)
        q_sum[:, cols] = mm(h_own[...], wq[0, :, cols])
        return 0

    lax.fori_loop(0, 4, q_own, 0)
    load_q1.wait()

    def q_oth(n, _):
        cols = pl.ds(pl.multiple_of(n * 256, 256), 256)
        q = (q_sum[:, cols] + mm(h_oth[...], wq[1, :, cols])).astype(jnp.bfloat16)
        g, pair = n // 2, lax.rem(n, 2)
        for blk in range(2):
            for j in range(2):
                first = pl.multiple_of((blk * 4 + pair * 2 + j) * BLK, BLK)
                qs[g, :, pl.ds(first, BLK)] = q[blk * BLK : (blk + 1) * BLK, j * HEAD : (j + 1) * HEAD].T
        return 0

    lax.fori_loop(0, 1, q_oth, 0)

    factor = math.log2(math.e) / math.sqrt(HEAD)

    def scores_of(slot, g, chunk, blocks, causal, first, last):
        q = qs[g, :, chunk * 256 : (chunk + 1) * 256]
        for i, (src, blk, _) in enumerate(blocks):
            s_buf[slot, i * BLK : (i + 1) * BLK] = mm(kv[src, 2 * blk + g, 0:128], q)

    def weights_of(slot, g, chunk, blocks, causal, first, last):
        lanes = slice(chunk * 256, (chunk + 1) * 256)
        low = low_row[0:1, lanes]
        parts = []
        for i, (_, blk, back) in enumerate(blocks):
            k_pos = ((here - back) * 2 + blk) * BLK + lax.broadcasted_iota(
                jnp.int32, (BLK, 256), 0
            )
            allowed = k_pos >= low
            if causal:
                allowed = allowed & (k_pos <= pos_row[0:1, lanes])
            parts.append(jnp.where(allowed, s_buf[slot, i * BLK : (i + 1) * BLK] * factor, NEG))
        top = functools.reduce(jnp.maximum, [p.reshape(BLK // 8, 8, 256).max(axis=0) for p in parts])
        top = jnp.max(top, axis=0, keepdims=True)
        if not first:
            old = m_s[g, 0:1, lanes]
            top = jnp.maximum(old, top)
            shrink = jnp.exp2(old - top)
            shrink_s[slot, 0:1] = shrink
        if not last:
            m_s[g, 0:1, lanes] = top
        total = None
        for i, s in enumerate(parts):
            p = jnp.exp2(s - top)
            p_buf[slot, i * BLK : (i + 1) * BLK] = p.astype(jnp.bfloat16)
            p = p.reshape(BLK // 8, 8, 256).sum(axis=0)
            total = p if total is None else total + p
        l_s[g, :, lanes] = total if first else total + l_s[g, :, lanes] * shrink

    def mix_of(slot, g, chunk, blocks, causal, first, last):
        lanes = slice(chunk * 256, (chunk + 1) * 256)
        values = jnp.concatenate([kv[src, 2 * blk + g, 128:256] for src, blk, _ in blocks], axis=1)
        mixed = mm(values, p_buf[slot, 0 : len(blocks) * BLK])
        if not first:
            mixed = mixed + acc_s[g, :, lanes] * shrink_s[slot, 0:1]
        if not last:
            acc_s[g, :, lanes] = mixed
            return
        mixed = mixed / jnp.sum(l_s[g, :, lanes], axis=0, keepdims=True)
        rows = slice(chunk // 2 * BLK, (chunk // 2 + 1) * BLK)
        for j in range(2):
            at = g * 4 + chunk % 2 * 2 + j
            out[rows, at * HEAD : (at + 1) * HEAD] = (
                mixed[:, j * HEAD : (j + 1) * HEAD].T.astype(jnp.bfloat16)
            )

    def run(tasks):
        count = len(tasks)
        for i in range(count + 2):
            for stage, j in ((scores_of, i), (mix_of, i - 2), (weights_of, i - 1)):
                if 0 <= j < count:
                    stage(j % 3, *tasks[j])

    def task(g, chunk, blocks, causal=False, first=False, last=False):
        return g, chunk, blocks, causal, first, last

    own = [(OWN, 0, 0), (OWN, 1, 0)]
    by_column(functools.partial(relay_first, 0))
    lax.fori_loop(1, 4, q_oth, 0)
    by_column(functools.partial(relay_first, 1))
    for i in range(2):
        run([task(i, chunk, own[: 1 + chunk // 2], causal=True, first=True) for chunk in range(4)])
        by_column(functools.partial(relay_second, i))
        by_column(functools.partial(relay_third, i))

    all_of([(BACK3, piece) for piece in range(4)] + [(BACK4, b) for b in B])
    back3 = [(BACK4, 1, 4), (BACK3, 0, 3), (BACK3, 1, 3)]
    run([task(g, chunk, back3[chunk // 2 * 2 :]) for g in range(2) for chunk in range(4)])
    all_of([(BACK1, piece) for piece in range(4)])
    back1 = [(BACK1, 0, 1), (BACK1, 1, 1)]
    run([task(g, chunk, back1) for g in range(2) for chunk in range(4)])
    back2 = [(BACK2, 0, 2), (BACK2, 1, 2)]
    for g in range(2):
        all_of([(BACK2, g), (BACK2, 2 + g)])
        run([task(g, chunk, back2, last=True) for chunk in range(4)])

    for swap in swaps:
        swap.wait_send()

    def finish(col):
        for kind in range(3):
            for k in range(sends[col][kind]):
                guarded(kind, lambda k=8 * kind + k: copy(OWN, BACK1, 0, up, k).wait_send())

    by_column(finish)


def local(hidden, block_owner, doc_lengths, w_query, w_key, value_weight):
    rows, half = hidden.shape
    q_cols, k_cols = w_query.shape[1], w_key.shape[1]
    groups = k_cols // HEAD
    shards = lax.axis_size("ctx")
    bf16, f32 = jnp.bfloat16, jnp.float32
    lanes = rows * q_cols // k_cols
    dma = pltpu.SemaphoreType.DMA
    any_spec = pl.BlockSpec(memory_space=pl.ANY)
    macs = rows * 2 * half * (q_cols + 2 * k_cols)
    return pl.pallas_call(
        functools.partial(kernel, shards),
        out_shape=pltpu.VMEM((rows, q_cols), bf16),
        in_specs=[any_spec] * 6,
        out_specs=pl.BlockSpec(memory_space=pltpu.VMEM),
        scratch_shapes=[
            pltpu.SMEM(block_owner.shape, jnp.int32),
            pltpu.SMEM(doc_lengths.shape, jnp.int32),
            pltpu.VMEM((rows, half), bf16),
            pltpu.VMEM((rows, half), bf16),
            pltpu.VMEM((2, half, q_cols), bf16),
            pltpu.VMEM((2, half, k_cols), bf16),
            pltpu.VMEM((2, half, k_cols), bf16),
            pltpu.VMEM((rows, 2 * k_cols), f32),
            pltpu.VMEM((rows, q_cols), f32),
            pltpu.VMEM((groups, HEAD, lanes), bf16),
            pltpu.VMEM((8, 4, 2 * BLK, HEAD), bf16),
            pltpu.VMEM((8, lanes), jnp.int32),
            pltpu.VMEM((8, lanes), jnp.int32),
            pltpu.VMEM((groups, 8, lanes), f32),
            pltpu.VMEM((groups, 8, lanes), f32),
            pltpu.VMEM((groups, HEAD, lanes), f32),
            pltpu.VMEM((3, 3 * BLK, 256), f32),
            pltpu.VMEM((3, 3 * BLK, 256), bf16),
            pltpu.VMEM((3, 8, 256), f32),
            dma((9,)),
            dma((2,)),
            dma((2,)),
            dma((24,)),
            dma((8, 4)),
        ],
        compiler_params=pltpu.CompilerParams(
            collective_id=0, has_side_effects=True, vmem_limit_bytes=56 << 20
        ),
        cost_estimate=pl.CostEstimate(
            flops=4 * macs, bytes_accessed=16 << 20, transcendentals=2 << 20
        ),
        name="attention",
    )(hidden, block_owner, doc_lengths, w_query, w_key, value_weight)


def solution(mesh):
    in_specs = (P("ctx", "head"), P(), P(), P(None, "head"), P(None, "head"), P(None, "head"))
    out_specs = P("ctx", "head")
    return jax.shard_map(local, mesh=mesh, in_specs=in_specs, out_specs=out_specs, check_vma=False)
```
